32 devices in a mesh: tok: 4 (over z), exp: 8 (over y, x, core).
Axes of the slice: x: 2, y: 2, z: 4, core: 2. Of those that a mesh axis runs over, the one named last changes fastest.
Arguments:
- x_rows: bfloat16 [768, 4096], P(('tok', 'exp')), may hold values from -6 to 6
- routes: int32 [768, 8], P(('tok', 'exp')), may hold values from 0 to 31, all different within a row; in each aligned block of 24 rows (0 to 23, 24 to 47, ...) at most 7 rows name the same one
- base_weight: bfloat16 [32, 1536, 4096], P('exp', 'tok'), may hold values from -6 to 6
- keep_mask: int32 [32, 24, 64], P('exp', 'tok'), may hold values 0 or 1
- dual_start: float32 [32, 1536, 4096], P('exp', 'tok'), may hold values from -4 to 4
Outputs:
- weight: float32 [32, 1536, 4096], P('exp', 'tok')
- dual: float32 [32, 1536, 4096], P('exp', 'tok')
The draws below stay inside these ranges and needn't reach their ends.
Inputs may be any that keep to these rules, and one draw needn't show every extreme that they name: `routes`: each row names 8 different experts; among the rows of one device no expert is named more than 7 times, a bound that some block reaches; every expert is named by at least one token.
All inputs are finite; a program needn't handle non-finite values. No bound on the sum of `keep_mask` on one device may be relied on, other than what follows from the above.
Results may differ from the reference program's by a relative error of at most 0.0027.
Values may be sent and summed in bfloat16 or wider, within the bound.
No kernel may reach another device: no remote copies, remote signals or barrier semaphores. Data moves between devices by JAX's collectives and lax.ppermute only.
A program may use at most 192 MiB of HBM per device.

```python
import math
import jax
import jax.numpy as jnp
import numpy as np
from jax import lax

D = 4096
HID = 1536
TOPK = 8
EXPERTS = 32
BLOCK = 64
ITERS = 2
ROWS_DEV = 24
TOKENS = 768
MOST = 7
DEVICES = 32


def place_ends(entries, rng, smallest, high):
    dims = entries.shape
    spot = [jax.random.randint(jax.random.fold_in(rng, axis), (), 0, dims[axis]) for axis in range(len(dims))]
    entries = entries.at[tuple(spot)].set(smallest)
    longest = dims.index(max(dims))
    spot[longest] = (spot[longest] + 1) % dims[longest]
    return entries.at[tuple(spot)].set(high)


def steps_of(key, dims, pieces, least, high):
    def one(axis_at, shards_of):
        heights = jax.random.uniform(jax.random.fold_in(jax.random.fold_in(key, 6), axis_at), (shards_of,), jnp.float32, least / len(pieces), high / len(pieces))
        return jnp.repeat(jnp.exp(heights), dims[axis_at] // shards_of).reshape((-1,) + (1,) * (len(dims) - axis_at - 1))

    level = one(*pieces[0])
    for cut in pieces[1:]:
        level = level * one(*cut)
    return level


def routed_block(stream_key, own, number, rows, number_of, top, most, lean):
    ranking = jax.random.permutation(stream_key, number_of)
    heavy_load, usual = portions_of(number_of, rows * top, most, lean, True), portions_of(number_of, rows * top, most, lean, False)
    places = jnp.arange(number_of)

    def named(tallies, rotation):
        used = int((tallies > 0).sum())
        fixed = max(1, used // 4)
        shifted = fixed + (places - fixed + rotation * (used - fixed)) % max(1, number_of - fixed)
        return jnp.zeros((number_of,), jnp.int32).at[ranking[jnp.where(places < fixed, places, shifted)]].set(jnp.asarray(tallies, jnp.int32))

    tallies = jnp.where(number % 4 == 0, named(heavy_load, number // 4), named(usual, number - number // 4 - 1))
    mixed = jax.random.permutation(jax.random.fold_in(own, 3), number_of)
    source_of, taker = mixed[0:number_of // 2 * 2:2], mixed[1:number_of // 2 * 2:2]
    margin = jnp.minimum(tallies[source_of] - 1, most - tallies[taker]) // 2
    margin = jnp.where((source_of == ranking[0]) | (taker == ranking[0]) | (tallies[taker] == 0), 0, jnp.maximum(margin, 0))
    shifted = jax.random.randint(jax.random.fold_in(own, 4), (number_of // 2,), 0, 1 << 20) % (margin + 1)
    tallies = tallies.at[source_of].add(-shifted).at[taker].add(shifted)
    members = jnp.searchsorted(jnp.cumsum(tallies), jnp.arange(rows * top), side="right").astype(jnp.int32)
    table = members.reshape(top, rows).T
    table = table[jax.random.permutation(jax.random.fold_in(own, 1), rows)]
    rotation = jax.random.randint(jax.random.fold_in(own, 2), (rows, 1), 0, top)
    return jnp.take_along_axis(table, (jnp.arange(top)[None, :] + rotation) % top, axis=1)


def portions_of(amount, total, limit, skew, full):
    portions = [(1 << 20) // math.isqrt(standing ** skew) + 1 for standing in range(1, amount + 1)]
    largest = limit if full else min(limit, max(-(-total // amount), total * portions[0] // sum(portions)))
    least = 1 if total - largest >= amount - 1 else 0
    holding, surplus = [largest] + [least] * (amount - 1), total - largest - least * (amount - 1)
    while surplus > 0:
        movable = [i for i in range(1, amount) if holding[i] < largest] or [i for i in range(1, amount) if holding[i] < limit]
        whole, left = sum([portions[i] for i in movable]), surplus
        for i in movable:
            more = min(limit - holding[i], max(1, left * portions[i] // whole), surplus)
            holding[i] = holding[i] + more
            surplus = surplus - more
    return np.array(holding)


def bell_draw(own_key, extent, deviation, limit, cuts=(), kind=jnp.bfloat16):
    result = jax.random.normal(own_key, extent, jnp.float32) * deviation
    if len(cuts) > 0:
        result = steps_of(own_key, extent, cuts, -0.22, 0.18) * result
    return jnp.clip(result, min=-limit, max=limit).astype(kind)


def setup_inputs(seed: int = 0) -> dict:
    seeds = jax.random.split(jax.random.key(seed), 6)
    x_rows = bell_draw(seeds[0], (TOKENS, D), 1.0, 6.0, ((0, 32),))
    routes_keys = jax.random.split(jax.random.fold_in(seeds[1], 1), TOKENS // ROWS_DEV)
    routes_turns = jax.random.permutation(jax.random.fold_in(seeds[1], 3), TOKENS // ROWS_DEV)
    routes = jax.vmap(lambda own, number: routed_block(jax.random.fold_in(seeds[1], 2), own, number, ROWS_DEV, EXPERTS, TOPK, MOST, 1))(routes_keys, routes_turns).reshape((TOKENS, TOPK))
    base_weight = bell_draw(seeds[2], (EXPERTS, HID, D), 1.0, 6.0, ((0, 8), (1, 4)))
    keep_mask = place_ends((jax.random.randint(seeds[3], (EXPERTS, HID // BLOCK, D // BLOCK), 0, 2) < 1).astype(jnp.int32), jax.random.fold_in(seeds[3], 1), 0, 1)
    dual_start = bell_draw(seeds[4], (EXPERTS, HID, D), 0.5, 4.0, ((0, 8), (1, 4)), jnp.float32)
    return dict(x_rows=x_rows, routes=routes, base_weight=base_weight, keep_mask=keep_mask, dual_start=dual_start)


step_rate = 0.2
penalty = 1.0


def reference(x_rows, routes, base_weight, keep_mask, dual_start):
    labels = jnp.arange(EXPERTS, dtype=jnp.int32)
    hits = jnp.any(routes[:, :, None] == labels[None, None, :], axis=1)
    capacity = DEVICES * MOST

    def one_expert(items):
        hit, base, keep, dual = items
        count_int = jnp.sum(hit.astype(jnp.int32))
        count = count_int.astype(jnp.float32)
        index = jnp.nonzero(hit, size=capacity, fill_value=0)[0].astype(jnp.int32)
        live = (jnp.arange(capacity, dtype=jnp.int32) < count_int).astype(jnp.bfloat16)
        rows = x_rows[index] * live[:, None]
        mask = jnp.repeat(jnp.repeat(keep.astype(jnp.float32), BLOCK, 0), BLOCK, 1)
        base32 = base.astype(jnp.float32)
        weight = mask * base32
        zed = weight
        for step in range(ITERS):
            delta = (weight - base32).astype(jnp.bfloat16)
            resid = jnp.dot(rows, delta.T, preferred_element_type=jnp.float32).astype(jnp.bfloat16)
            grad = jnp.dot(resid.T, rows, preferred_element_type=jnp.float32) / count
            weight = weight - step_rate * (grad + penalty * (weight - zed + dual))
            zed = mask * (weight + dual)
            dual = dual + weight - zed
        return weight, dual

    weight, dual = lax.map(one_expert, (hits.T, base_weight, keep_mask, dual_start))
    return weight, dual
```

```python
import functools

import jax
import jax.numpy as jnp
from jax import lax
from jax.experimental import pallas as pl
from jax.experimental.pallas import tpu as pltpu
from jax.sharding import PartitionSpec as P

EXPERTS = 32
BLOCK = 64
ROWS_BLOCK = 24
MOST = 7
LANES = 128

step_rate = 0.2

F32 = jnp.float32
BF16 = jnp.bfloat16


def dot_nn(a, b):
    return jnp.dot(a, b, preferred_element_type=F32)


def dot_nt(a, b):
    return lax.dot_general(a, b, (((1,), (1,)), ((), ())), preferred_element_type=F32)


def kernel(
    chunk, width, topk, first_ref, x_ref, base_ref, dual_ref, mask_ref,
    weight_out, dual_out, rows, rank, hits, scale,
):
    expert, tile = pl.program_id(0), pl.program_id(1)
    tokens = x_ref.shape[0]
    slots = rows.shape[0]
    count_here = hits.shape[0]
    tall = base_ref.shape[1]
    cuts = [pl.ds(start, chunk) for start in range(0, width, chunk)]

    @pl.when((expert == 0) & (tile == 0))
    def _():
        named = x_ref[:, pl.ds(width, LANES)].astype(F32).T[:topk, :]
        for own in range(count_here):
            label = (first_ref[0] + own).astype(F32)
            hit = jnp.max(jnp.where(named == label, 1.0, 0.0), axis=0, keepdims=True)
            hits[own : own + 1, :] = hit
        earlier = lax.broadcasted_iota(jnp.int32, (tokens, tokens), 0)
        later = lax.broadcasted_iota(jnp.int32, (tokens, tokens), 1)
        ahead = jnp.where(earlier < later, 1.0, 0.0).astype(BF16)
        rank[...] = dot_nn(hits[...].astype(BF16), ahead)

    @pl.when(tile == 0)
    def _():
        hit = hits[pl.ds(expert, 1), :]
        place = rank[pl.ds(expert, 1), :]
        slot = lax.broadcasted_iota(jnp.int32, (slots, tokens), 0).astype(F32)
        taken = jnp.where((slot == place) & (hit > 0.5), 1.0, 0.0).astype(BF16)
        for cut in cuts:
            rows[:, cut] = dot_nn(taken, x_ref[:, cut]).astype(BF16)
        total = jnp.sum(hit, axis=1, keepdims=True)
        scale[...] = jnp.broadcast_to(step_rate / total, scale.shape)

    rate = scale[0:1, 0:1]
    parts = [slice(start, start + BLOCK) for start in range(0, tall, BLOCK)]

    resid = jnp.zeros((tall, slots), F32)
    for cut in cuts:
        delta = jnp.concatenate(
            [base_ref[0, part, cut] * (mask_ref[0, 0, i : i + 1, cut] - 1.0).astype(BF16) for i, part in enumerate(parts)],
            axis=0,
        )
        resid = resid + dot_nt(delta, rows[:, cut])
    resid = resid.astype(BF16)

    after = jnp.zeros((tall, slots), F32)
    for cut in cuts:
        grad = dot_nn(resid, rows[:, cut])
        deltas = []
        for i, part in enumerate(parts):
            keep = mask_ref[0, 0, i : i + 1, cut]
            base = base_ref[0, part, cut].astype(F32)
            weight = keep * base - step_rate * dual_ref[0, part, cut] - rate * grad[part, :]
            weight_out[0, part, cut] = weight
            deltas.append((weight - base).astype(BF16))
        after = after + dot_nt(jnp.concatenate(deltas, axis=0), rows[:, cut])
    resid = after.astype(BF16)

    for cut in cuts:
        grad = dot_nn(resid, rows[:, cut])
        for i, part in enumerate(parts):
            keep = mask_ref[0, 0, i : i + 1, cut]
            weight = weight_out[0, part, cut]
            both = weight + dual_ref[0, part, cut]
            weight = (1.0 - step_rate) * weight - (step_rate - 2.0 * step_rate * keep) * both - rate * grad[part, :]
            weight_out[0, part, cut] = weight
            dual_out[0, part, cut] = (1.0 - keep) * (both + weight)


def fused(first, gathered, base_weight, mask, dual_start, topk, tall):
    local, hidden, width = base_weight.shape
    tokens = gathered.shape[0]
    slots = -(-tokens // ROWS_BLOCK) * MOST
    slots = -(-min(slots, tokens) // 16) * 16
    tiles = hidden // tall
    block = pl.BlockSpec((1, tall, width), lambda e, t: (e, t, 0))
    out = jax.ShapeDtypeStruct(dual_start.shape, F32)
    macs = local * slots * width * (4 * hidden + tokens)
    return pl.pallas_call(
        functools.partial(kernel, 512, width, topk),
        grid=(local, tiles),
        in_specs=[
            pl.BlockSpec(memory_space=pltpu.SMEM),
            pl.BlockSpec(gathered.shape, lambda e, t: (0, 0), pipeline_mode=pl.Buffered(1)),
            block,
            block,
            pl.BlockSpec((1, 1, tall // BLOCK, width), lambda e, t: (e, t, 0, 0)),
        ],
        out_specs=[block, block],
        out_shape=[out, out],
        scratch_shapes=[
            pltpu.VMEM((slots, width), BF16),
            pltpu.VMEM((local, tokens), F32),
            pltpu.VMEM((local, tokens), F32),
            pltpu.VMEM((8, LANES), F32),
        ],
        compiler_params=pltpu.CompilerParams(
            vmem_limit_bytes=60 * 1024 * 1024,
            dimension_semantics=("arbitrary", "arbitrary"),
        ),
        cost_estimate=pl.CostEstimate(flops=2 * macs, bytes_accessed=14 * base_weight.size + 2 * gathered.size, transcendentals=0),
    )(first, gathered, base_weight, dual_start, mask)


def on_device(x_rows, routes, base_weight, keep_mask, dual_start):
    local, hidden, width = base_weight.shape
    topk = routes.shape[1]
    tall = 3 * BLOCK
    with jax.named_scope("gather_rows"):
        named = jnp.pad(routes.astype(BF16), ((0, 0), (0, LANES - topk)))
        own = jnp.concatenate([x_rows, named], axis=1)
        gathered = lax.all_gather(own, ("tok", "exp"), axis=0, tiled=True)
    mask = jnp.repeat(keep_mask.astype(F32), BLOCK, 2)
    mask = mask.reshape(local, hidden // tall, tall // BLOCK, width)
    first = (lax.axis_index("exp") * local).astype(jnp.int32).reshape(1)
    with jax.named_scope("fused_iterations"):
        return fused(first, gathered, base_weight, mask, dual_start, topk, tall)


def solution(mesh):
    return jax.shard_map(
        on_device,
        mesh=mesh,
        in_specs=(
            P(("tok", "exp"), None),
            P(("tok", "exp"), None),
            P("exp", "tok", None),
            P("exp", "tok", None),
            P("exp", "tok", None),
        ),
        out_specs=(P("exp", "tok", None), P("exp", "tok", None)),
        check_vma=False,
    )
```

```python
import functools

import jax
import jax.numpy as jnp
from jax import lax
from jax.experimental import pallas as pl
from jax.experimental.pallas import tpu as pltpu
from jax.sharding import PartitionSpec as P

EXPERTS = 32
BLOCK = 64
ROWS_BLOCK = 24
MOST = 7
LANES = 128
MIB = 1024 * 1024

step_rate = 0.2

F32 = jnp.float32
BF16 = jnp.bfloat16


def dot_nn(a, b):
    return jnp.dot(a, b, preferred_element_type=F32)


def dot_nt(a, b):
    return lax.dot_general(a, b, (((1,), (1,)), ((), ())), preferred_element_type=F32)


def cuts_of(width, chunk):
    return [pl.ds(start, chunk) for start in range(0, width, chunk)]


def pack_kernel(n_pieces, half, topk, chunk, *refs):
    pieces, refs = refs[:n_pieces], refs[n_pieces:]
    if half == 0:
        first_ref, base_ref, mask_ref, rows_out, resid_out, hits, rank, rate_out, gathered, sems = refs
    else:
        hits, rank, part_ref, base_ref, mask_ref, rows_out, resid_out, gathered, sems = refs
    expert = pl.program_id(0)
    tokens = gathered.shape[0]
    slots, width = rows_out.shape[1], rows_out.shape[2]
    local = hits.shape[0]
    tall = base_ref.shape[1]
    piece_rows = tokens // n_pieces

    @pl.when(expert == 0)
    def _():
        copies = [
            pltpu.make_async_copy(piece, gathered.at[pl.ds(i * piece_rows, piece_rows), :], sems.at[i])
            for i, piece in enumerate(pieces)
        ]
        for copy in copies:
            copy.start()
        for copy in copies:
            copy.wait()
        if half == 0:
            named = gathered[:, pl.ds(width, LANES)].astype(F32).T[:topk, :]
            for own in range(local):
                label = (first_ref[0] + own).astype(F32)
                hit = jnp.max(jnp.where(named == label, 1.0, 0.0), axis=0, keepdims=True)
                hits[own : own + 1, :] = hit
                total = jnp.sum(hit, axis=1, keepdims=True)
                rate_out[own : own + 1, :] = jnp.broadcast_to(step_rate / total, (1, LANES))
            earlier = lax.broadcasted_iota(jnp.int32, (tokens, tokens), 0)
            later = lax.broadcasted_iota(jnp.int32, (tokens, tokens), 1)
            ahead = jnp.where(earlier < later, 1.0, 0.0).astype(BF16)
            rank[...] = dot_nn(hits[...].astype(BF16), ahead)

    hit = hits[pl.ds(expert, 1), :]
    place = rank[pl.ds(expert, 1), :]
    slot = lax.broadcasted_iota(jnp.int32, (slots, tokens), 0).astype(F32)
    taken = jnp.where((slot == place) & (hit > 0.5), 1.0, 0.0).astype(BF16)
    resid = jnp.zeros((tall, slots), F32) if half == 0 else part_ref[0]
    for cut in cuts_of(width, chunk):
        rows = dot_nn(taken, gathered[:, cut]).astype(BF16)
        rows_out[0, :, cut] = rows
        delta = jnp.concatenate(
            [
                base_ref[0, start : start + BLOCK, cut] * (mask_ref[0, i : i + 1, cut] - 1.0).astype(BF16)
                for i, start in enumerate(range(0, tall, BLOCK))
            ],
            axis=0,
        )
        resid = resid + dot_nt(delta, rows)
    resid_out[0] = resid.astype(resid_out.dtype)


def pack(half, halves, pieces, extra, base_weight, mask, slots, topk):
    local, hidden, width = base_weight.shape
    part = width // halves
    n_pieces = len(pieces)
    piece_rows, piece_width = pieces[0].shape
    tokens = n_pieces * piece_rows
    last = half == halves - 1
    small = pl.BlockSpec((local, tokens), lambda e: (0, 0))
    resid = pl.BlockSpec((1, hidden, slots), lambda e: (e, 0, 0))
    in_specs = [pl.BlockSpec(memory_space=pl.ANY)] * n_pieces
    if half == 0:
        in_specs += [pl.BlockSpec(memory_space=pltpu.SMEM)]
    else:
        in_specs += [small, small, resid]
    in_specs += [
        pl.BlockSpec((1, hidden, part), lambda e: (e, 0, half)),
        pl.BlockSpec((1, hidden // BLOCK, part), lambda e: (e, 0, half)),
    ]
    out_specs = [pl.BlockSpec((1, slots, part), lambda e: (e, 0, 0)), resid]
    out_shape = [
        jax.ShapeDtypeStruct((local, slots, part), BF16),
        jax.ShapeDtypeStruct((local, hidden, slots), BF16 if last else F32),
    ]
    if half == 0:
        out_specs += [small, small, pl.BlockSpec((local, LANES), lambda e: (0, 0))]
        out_shape += [jax.ShapeDtypeStruct((local, tokens), F32)] * 2
        out_shape += [jax.ShapeDtypeStruct((local, LANES), F32)]
    macs = local * slots * part * (hidden + tokens)
    return pl.pallas_call(
        functools.partial(pack_kernel, n_pieces, half, topk, 512),
        grid=(local,),
        in_specs=in_specs,
        out_specs=out_specs,
        out_shape=out_shape,
        scratch_shapes=[pltpu.VMEM((tokens, piece_width), BF16), pltpu.SemaphoreType.DMA((n_pieces,))],
        compiler_params=pltpu.CompilerParams(vmem_limit_bytes=48 * MIB, dimension_semantics=("arbitrary",)),
        cost_estimate=pl.CostEstimate(
            flops=2 * macs, bytes_accessed=2 * (tokens + local * (slots + hidden)) * part, transcendentals=0
        ),
    )(*pieces, *extra, base_weight, mask)


def main_kernel(halves, chunk, rate_ref, resid_ref, *refs):
    rows_refs, (base_ref, dual_ref, mask_ref, weight_out, dual_out) = refs[:halves], refs[halves:]
    tall = base_ref.shape[1]
    slots, part_width = rows_refs[0].shape[1:]
    rate = rate_ref[pl.ds(pl.program_id(0), 1), 0:1]
    parts = [slice(start, start + BLOCK) for start in range(0, tall, BLOCK)]
    cuts = [
        (rows_refs[h], cut, pl.ds(h * part_width + cut.start, chunk))
        for h in range(halves)
        for cut in cuts_of(part_width, chunk)
    ]

    resid = resid_ref[0]
    after = jnp.zeros((tall, slots), F32)
    for rows, here, cut in cuts:
        grad = dot_nn(resid, rows[0, :, here])
        deltas = []
        for i, part in enumerate(parts):
            keep = mask_ref[0, 0, i : i + 1, cut]
            base = base_ref[0, part, cut].astype(F32)
            weight = keep * base - step_rate * dual_ref[0, part, cut] - rate * grad[part, :]
            weight_out[0, part, cut] = weight
            deltas.append((weight - base).astype(BF16))
        after = after + dot_nt(jnp.concatenate(deltas, axis=0), rows[0, :, here])
    resid = after.astype(BF16)

    for rows, here, cut in cuts:
        grad = dot_nn(resid, rows[0, :, here])
        for i, part in enumerate(parts):
            keep = mask_ref[0, 0, i : i + 1, cut]
            weight = weight_out[0, part, cut]
            both = weight + dual_ref[0, part, cut]
            weight = (1.0 - step_rate) * weight - (step_rate - 2.0 * step_rate * keep) * both - rate * grad[part, :]
            weight_out[0, part, cut] = weight
            dual_out[0, part, cut] = (1.0 - keep) * (both + weight)


def iterate(rate, resid, rows, base_weight, mask, dual_start, tall):
    local, hidden, width = base_weight.shape
    slots, part = rows[0].shape[1:]
    tiles = hidden // tall
    block = pl.BlockSpec((1, tall, width), lambda e, t: (e, t, 0))
    out = jax.ShapeDtypeStruct(dual_start.shape, F32)
    macs = local * slots * width * 3 * hidden
    mask = mask.reshape(local, tiles, tall // BLOCK, width)
    return pl.pallas_call(
        functools.partial(main_kernel, len(rows), 512),
        grid=(local, tiles),
        in_specs=[pl.BlockSpec(rate.shape, lambda e, t: (0, 0)), pl.BlockSpec((1, tall, slots), lambda e, t: (e, t, 0))]
        + [pl.BlockSpec((1, slots, part), lambda e, t: (e, 0, 0)) for _ in rows]
        + [block, block, pl.BlockSpec((1, 1, tall // BLOCK, width), lambda e, t: (e, t, 0, 0))],
        out_specs=[block, block],
        out_shape=[out, out],
        compiler_params=pltpu.CompilerParams(
            vmem_limit_bytes=56 * MIB, dimension_semantics=("arbitrary", "arbitrary")
        ),
        cost_estimate=pl.CostEstimate(flops=2 * macs, bytes_accessed=14 * base_weight.size, transcendentals=0),
    )(rate, resid, *rows, base_weight, dual_start, mask)


def spread(own, bits):
    n_tok, n_exp = lax.axis_size("tok"), lax.axis_size("exp")
    column = [own]
    for shift in range(1, n_tok):
        column.append(lax.ppermute(own, "tok", [(i, (i + shift) % n_tok) for i in range(n_tok)]))
    pieces = {0: jnp.concatenate(column, axis=0)}
    for bit in bits:
        swap = [(i, i ^ (1 << bit)) for i in range(n_exp)]
        pieces.update({at ^ (1 << bit): lax.ppermute(piece, "exp", swap) for at, piece in pieces.items()})
    return [pieces[i] for i in range(n_exp)]


def on_device(x_rows, routes, base_weight, keep_mask, dual_start):
    local, hidden, width = base_weight.shape
    topk = routes.shape[1]
    n_tok, n_exp = lax.axis_size("tok"), lax.axis_size("exp")
    tokens = n_tok * n_exp * x_rows.shape[0]
    slots = -(-tokens // ROWS_BLOCK) * MOST
    slots = -(-min(slots, tokens) // 16) * 16
    halves = 2
    part = width // halves
    top = n_exp.bit_length() - 1
    assert 1 << top == n_exp
    named = jnp.pad(routes.astype(BF16), ((0, 0), (0, LANES - topk)))
    sent = [x_rows[:, h * part : (h + 1) * part] for h in range(halves)]
    sent[0] = jnp.concatenate([sent[0], named], axis=1)
    orders = [list(range(1, top)) + [0], list(range(1, top))[::-1] + [0]]
    with jax.named_scope("exchange_rows"):
        pieces = [spread(own, orders[h % 2]) for h, own in enumerate(sent)]
    mask = jnp.repeat(keep_mask.astype(F32), BLOCK, 2)
    first = (lax.axis_index("exp") * local).astype(jnp.int32).reshape(1)
    rows = []
    with jax.named_scope("pack_rows"):
        part_rows, resid, hits, rank, rate = pack(0, halves, pieces[0], [first], base_weight, mask, slots, topk)
        rows.append(part_rows)
        for h in range(1, halves):
            part_rows, resid = pack(h, halves, pieces[h], [hits, rank, resid], base_weight, mask, slots, topk)
            rows.append(part_rows)
    with jax.named_scope("iterations"):
        return iterate(rate, resid, rows, base_weight, mask, dual_start, 3 * BLOCK)


def solution(mesh):
    return jax.shard_map(
        on_device,
        mesh=mesh,
        in_specs=(
            P(("tok", "exp"), None),
            P(("tok", "exp"), None),
            P("exp", "tok", None),
            P("exp", "tok", None),
            P("exp", "tok", None),
        ),
        out_specs=(P("exp", "tok", None), P("exp", "tok", None)),
        check_vma=False,
    )
```

```python
import functools

import jax
import jax.numpy as jnp
from jax import lax
from jax.experimental import pallas as pl
from jax.experimental.pallas import tpu as pltpu
from jax.sharding import PartitionSpec as P

EXPERTS = 32
BLOCK = 64
ROWS_BLOCK = 24
MOST = 7
LANES = 128
MIB = 1024 * 1024
SPARE = 4

step_rate = 0.2

F32 = jnp.float32
BF16 = jnp.bfloat16


def dot_nn(a, b):
    return jnp.dot(a, b, preferred_element_type=F32)


def dot_nt(a, b):
    return lax.dot_general(a, b, (((1,), (1,)), ((), ())), preferred_element_type=F32)


def cuts_of(width, chunk):
    return [pl.ds(start, chunk) for start in range(0, width, chunk)]


def load_kernel(n_marks, *refs):
    base_ref, dual_ref, base_out, dual_out, sems = refs[n_marks:]
    copies = [
        pltpu.make_async_copy(base_ref, base_out, sems.at[0]),
        pltpu.make_async_copy(dual_ref, dual_out, sems.at[1]),
    ]
    for copy in copies:
        copy.start()
    for copy in copies:
        copy.wait()


def load(marks, base_weight, dual_start):
    anywhere = pl.BlockSpec(memory_space=pl.ANY)
    return pl.pallas_call(
        functools.partial(load_kernel, len(marks)),
        in_specs=[anywhere] * (len(marks) + 2),
        out_specs=[anywhere, anywhere],
        out_shape=[pltpu.VMEM(x.shape, x.dtype) for x in (base_weight, dual_start)],
        scratch_shapes=[pltpu.SemaphoreType.DMA((2,))],
        compiler_params=pltpu.CompilerParams(vmem_limit_bytes=16 * MIB),
        cost_estimate=pl.CostEstimate(flops=0, bytes_accessed=6 * base_weight.size, transcendentals=0),
    )(*marks, base_weight, dual_start)


def fused_kernel(chunk, topk, halves, *refs):
    gathered, (base_ref, dual_ref, keep_ref, weight_out, dual_out, rows, rank, hits, scale, mask) = refs[:halves], refs[halves:]
    expert, tile = pl.program_id(0), pl.program_id(1)
    tokens = gathered[0].shape[0]
    slots, width = rows.shape
    part_width = width // halves
    local = hits.shape[0]
    tall = weight_out.shape[1]
    blocks = tall // BLOCK
    cuts = cuts_of(width, chunk)

    @pl.when((expert == 0) & (tile == 0))
    def _():
        named = gathered[0][:, pl.ds(part_width, LANES)].astype(F32).T[:topk, :]
        for own in range(local):
            label = (lax.axis_index("exp") * local + own).astype(F32)
            hits[own : own + 1, :] = jnp.max(jnp.where(named == label, 1.0, 0.0), axis=0, keepdims=True)
        earlier = lax.broadcasted_iota(jnp.int32, (tokens, tokens), 0)
        later = lax.broadcasted_iota(jnp.int32, (tokens, tokens), 1)
        ahead = jnp.where(earlier < later, 1.0, 0.0).astype(BF16)
        rank[...] = dot_nn(hits[...].astype(BF16), ahead)
        count = keep_ref.shape[2]
        at = lax.broadcasted_iota(jnp.int32, (count, width), 0) * BLOCK
        column = lax.broadcasted_iota(jnp.int32, (count, width), 1)
        wide = jnp.where((column >= at) & (column < at + BLOCK), 1.0, 0.0).astype(BF16)
        for own in range(local):
            mask[own] = dot_nn(keep_ref[own].astype(F32).astype(BF16), wide)

    @pl.when(tile == 0)
    def _():
        hit = hits[pl.ds(expert, 1), :]
        place = rank[pl.ds(expert, 1), :]
        slot = lax.broadcasted_iota(jnp.int32, (slots, tokens), 0).astype(F32)
        taken = jnp.where((slot == place) & (hit > 0.5), 1.0, 0.0).astype(BF16)
        for cut in cuts:
            half, start = divmod(cut.start, part_width)
            rows[:, cut] = dot_nn(taken, gathered[half][:, pl.ds(start, chunk)]).astype(BF16)
        total = jnp.sum(hit, axis=1, keepdims=True)
        scale[...] = jnp.broadcast_to(step_rate / total, scale.shape)

    rate = scale[0:1, 0:1]
    parts = [slice(start, start + BLOCK) for start in range(0, tall, BLOCK)]
    sources = [pl.ds(pl.multiple_of(tile * tall + part.start, BLOCK), BLOCK) for part in parts]
    keeps = [pl.ds(tile * blocks + i, 1) for i in range(blocks)]

    resid = jnp.zeros((tall, slots), F32)
    for cut in cuts:
        deltas = [
            base_ref[expert, source, cut] * (mask[expert, at, cut] - 1.0).astype(BF16)
            for source, at in zip(sources, keeps)
        ]
        resid = resid + dot_nt(jnp.concatenate(deltas, axis=0), rows[:, cut])
    resid = resid.astype(BF16)

    after = jnp.zeros((tall, slots), F32)
    for cut in cuts:
        grad = dot_nn(resid, rows[:, cut])
        deltas = []
        for part, source, at in zip(parts, sources, keeps):
            base = base_ref[expert, source, cut].astype(F32)
            weight = mask[expert, at, cut] * base - step_rate * dual_ref[expert, source, cut] - rate * grad[part, :]
            weight_out[0, part, cut] = weight
            deltas.append((weight - base).astype(BF16))
        after = after + dot_nt(jnp.concatenate(deltas, axis=0), rows[:, cut])
    resid = after.astype(BF16)

    for cut in cuts:
        grad = dot_nn(resid, rows[:, cut])
        for part, source, at in zip(parts, sources, keeps):
            keep = mask[expert, at, cut]
            weight = weight_out[0, part, cut]
            both = weight + dual_ref[expert, source, cut]
            weight = (1.0 - step_rate) * weight - (step_rate - 2.0 * step_rate * keep) * both - rate * grad[part, :]
            weight_out[0, part, cut] = weight
            dual_out[0, part, cut] = (1.0 - keep) * (both + weight)


def fused(gathered, base_weight, keep_mask, dual_start, topk, tall):
    local, hidden, width = base_weight.shape
    tokens = gathered[0].shape[0]
    slots = -(-tokens // ROWS_BLOCK) * MOST
    slots = -(-min(slots, tokens) // 16) * 16
    block = pl.BlockSpec((1, tall, width), lambda e, t: (e, t, 0))
    whole = pl.BlockSpec(memory_space=pltpu.VMEM)
    out = jax.ShapeDtypeStruct(dual_start.shape, F32)
    scoped = 16 * tall * width + 2 * slots * (width + 2 * tokens) + 32 * local * width + SPARE * MIB
    macs = local * slots * width * (4 * hidden + tokens)
    held = [pltpu.with_memory_space_constraint(x, pltpu.VMEM) for x in (*gathered, base_weight, dual_start)]
    return pl.pallas_call(
        functools.partial(fused_kernel, 512, topk, len(gathered)),
        grid=(local, hidden // tall),
        in_specs=[whole] * len(held) + [whole],
        out_specs=[block, block],
        out_shape=[out, out],
        scratch_shapes=[
            pltpu.VMEM((slots, width), BF16),
            pltpu.VMEM((local, tokens), F32),
            pltpu.VMEM((local, tokens), F32),
            pltpu.VMEM((8, LANES), F32),
            pltpu.VMEM((local, keep_mask.shape[1], width), F32),
        ],
        compiler_params=pltpu.CompilerParams(
            vmem_limit_bytes=scoped, dimension_semantics=("arbitrary", "arbitrary")
        ),
        cost_estimate=pl.CostEstimate(flops=2 * macs, bytes_accessed=8 * base_weight.size, transcendentals=0),
    )(*held, keep_mask)


def spread(own):
    n_tok, n_exp = lax.axis_size("tok"), lax.axis_size("exp")
    top = n_exp.bit_length() - 1
    assert 1 << top == n_exp

    def swap(piece, bit):
        return lax.ppermute(piece, "exp", [(i, i ^ (1 << bit)) for i in range(n_exp)])

    column = [own]
    for shift in range(1, n_tok):
        column.append(lax.ppermute(own, "tok", [(i, (i + shift) % n_tok) for i in range(n_tok)]))
    pieces = {0: jnp.concatenate(column, axis=0)}
    if top == 3:
        one, two = swap(pieces[0], 1), swap(pieces[0], 2)
        middle = own.shape[1] // 2 // LANES * LANES
        far = jnp.concatenate([swap(one[:, :middle], 2), swap(two[:, middle:], 1)], axis=1)
        pieces.update({2: one, 4: two, 6: far})
    else:
        for bit in range(1, top):
            pieces.update({at ^ (1 << bit): swap(piece, bit) for at, piece in pieces.items()})
    pieces.update({at ^ 1: swap(piece, 0) for at, piece in pieces.items()})
    return jnp.concatenate([pieces[i] for i in range(n_exp)], axis=0), [pieces[i] for i in range(n_exp) if i.bit_count() == 1 and i > 1]


def on_device(x_rows, routes, base_weight, keep_mask, dual_start):
    local, hidden, width = base_weight.shape
    topk = routes.shape[1]
    halves = 2
    part = width // halves
    named = jnp.pad(routes.astype(BF16), ((0, 0), (0, LANES - topk)))
    sent = [x_rows[:, h * part : (h + 1) * part] for h in range(halves)]
    sent[0] = jnp.concatenate([sent[0], named], axis=1)
    with jax.named_scope("exchange_rows"):
        gathered, marks = zip(*[spread(own) for own in sent])
    with jax.named_scope("load_weights"):
        base_weight, dual_start = load(marks[-1], base_weight, dual_start)
    tall = 2 * BLOCK if hidden % (2 * BLOCK) == 0 else BLOCK
    with jax.named_scope("fused_iterations"):
        return fused(gathered, base_weight, keep_mask, dual_start, topk, tall)


def solution(mesh):
    return jax.shard_map(
        on_device,
        mesh=mesh,
        in_specs=(
            P(("tok", "exp"), None),
            P(("tok", "exp"), None),
            P("exp", "tok", None),
            P("exp", "tok", None),
            P("exp", "tok", None),
        ),
        out_specs=(P("exp", "tok", None), P("exp", "tok", None)),
        check_vma=False,
    )
```

```python
import functools

import jax
import jax.numpy as jnp
from jax import lax
from jax.experimental import pallas as pl
from jax.experimental.pallas import tpu as pltpu
from jax.sharding import PartitionSpec as P

EXPERTS = 32
BLOCK = 64
ROWS_BLOCK = 24
MOST = 7
ITERS = 2
LANES = 128
MIB = 1024 * 1024
SPARE = 6

step_rate = 0.2

F32 = jnp.float32
BF16 = jnp.bfloat16


def dot_nn(a, b):
    return jnp.dot(a, b, preferred_element_type=F32)


def dot_nt(a, b):
    return lax.dot_general(a, b, (((1,), (1,)), ((), ())), preferred_element_type=F32)


def cuts_of(width, chunk):
    return [pl.ds(start, chunk) for start in range(0, width, chunk)]


def load_kernel(n_marks, *refs):
    base_ref, dual_ref, base_out, dual_out, sems = refs[n_marks:]
    copies = [
        pltpu.make_async_copy(base_ref, base_out, sems.at[0]),
        pltpu.make_async_copy(dual_ref, dual_out, sems.at[1]),
    ]
    for copy in copies:
        copy.start()
    for copy in copies:
        copy.wait()


def load(marks, base_weight, dual_start):
    anywhere = pl.BlockSpec(memory_space=pl.ANY)
    return pl.pallas_call(
        functools.partial(load_kernel, len(marks)),
        in_specs=[anywhere] * (len(marks) + 2),
        out_specs=[anywhere, anywhere],
        out_shape=[pltpu.VMEM(x.shape, x.dtype) for x in (base_weight, dual_start)],
        scratch_shapes=[pltpu.SemaphoreType.DMA((2,))],
        compiler_params=pltpu.CompilerParams(vmem_limit_bytes=16 * MIB),
        cost_estimate=pl.CostEstimate(flops=0, bytes_accessed=6 * base_weight.size, transcendentals=0),
    )(*marks, base_weight, dual_start)


def fused_kernel(chunk, topk, halves, *refs):
    gathered = refs[:halves]
    base_ref, _, keep_ref, weight_hbm, dual_hbm, dual, *refs = refs[halves:]
    rows, across, held, rank, hits, mask, weight_sems, dual_sems = refs
    expert = pl.program_id(0)
    tokens = gathered[0].shape[0]
    slots, width = rows.shape
    part_width = width // halves
    local, tall, _ = base_ref.shape
    cuts = cuts_of(width, chunk)
    parts = [slice(start, start + BLOCK) for start in range(0, tall, BLOCK)]

    def weight_copy(at, i):
        return pltpu.make_async_copy(held.at[:, cuts[i]], weight_hbm.at[at, :, cuts[i]], weight_sems.at[i])

    def dual_copy(at, i):
        return pltpu.make_async_copy(dual.at[at, :, cuts[i]], dual_hbm.at[at, :, cuts[i]], dual_sems.at[at, i])

    @pl.when(expert == 0)
    def _():
        named = gathered[0][:, pl.ds(part_width, LANES)].astype(F32).T[:topk, :]
        for own in range(local):
            label = (lax.axis_index("exp") * local + own).astype(F32)
            hits[own : own + 1, :] = jnp.max(jnp.where(named == label, 1.0, 0.0), axis=0, keepdims=True)
        earlier = lax.broadcasted_iota(jnp.int32, (tokens, tokens), 0)
        later = lax.broadcasted_iota(jnp.int32, (tokens, tokens), 1)
        ahead = jnp.where(earlier < later, 1.0, 0.0).astype(BF16)
        rank[...] = dot_nn(hits[...].astype(BF16), ahead)
        count = keep_ref.shape[2]
        at = lax.broadcasted_iota(jnp.int32, (count, width), 0) * BLOCK
        column = lax.broadcasted_iota(jnp.int32, (count, width), 1)
        wide = jnp.where((column >= at) & (column < at + BLOCK), 1.0, 0.0).astype(BF16)
        for own in range(local):
            mask[own] = dot_nn(keep_ref[own].astype(F32).astype(BF16), wide)

    hit = hits[pl.ds(expert, 1), :]
    place = rank[pl.ds(expert, 1), :]
    slot = lax.broadcasted_iota(jnp.int32, (slots, tokens), 0).astype(F32)
    taken = jnp.where((slot == place) & (hit > 0.5), 1.0, 0.0).astype(BF16)
    rate = step_rate / jnp.sum(hit, axis=1, keepdims=True)
    resid = jnp.zeros((tall, slots), F32)
    for cut in cuts:
        half, start = divmod(cut.start, part_width)
        picked = dot_nn(taken, gathered[half][:, pl.ds(start, chunk)])
        rows[:, cut] = picked.astype(BF16)
        across[cut, :] = picked.T.astype(BF16)
        deltas = [
            base_ref[expert, part, cut] * (mask[expert, i : i + 1, cut] - 1.0).astype(BF16) for i, part in enumerate(parts)
        ]
        resid = resid + dot_nn(jnp.concatenate(deltas, axis=0), across[cut, :])
    resid = resid.astype(BF16)

    @pl.when(expert > 0)
    def _():
        for i in range(len(cuts)):
            weight_copy(expert - 1, i).wait()

    after = jnp.zeros((tall, slots), F32)
    for cut in cuts:
        grad = dot_nn(resid, rows[:, cut])
        deltas = []
        for i, part in enumerate(parts):
            base = base_ref[expert, part, cut].astype(F32)
            weight = mask[expert, i : i + 1, cut] * base - step_rate * dual[expert, part, cut] - rate * grad[part, :]
            held[part, cut] = weight
            deltas.append((weight - base).astype(BF16))
        after = after + dot_nn(jnp.concatenate(deltas, axis=0), across[cut, :])
    resid = after.astype(BF16)

    for n, cut in enumerate(cuts):
        grad = dot_nn(resid, rows[:, cut])
        for i, part in enumerate(parts):
            keep = mask[expert, i : i + 1, cut]
            weight = held[part, cut]
            both = weight + dual[expert, part, cut]
            weight = (1.0 - step_rate) * weight - (step_rate - 2.0 * step_rate * keep) * both - rate * grad[part, :]
            held[part, cut] = weight
            dual[expert, part, cut] = (1.0 - keep) * (both + weight)
        weight_copy(expert, n).start()
        dual_copy(expert, n).start()

    @pl.when(expert == local - 1)
    def _():
        for i in range(len(cuts)):
            weight_copy(expert, i).wait()
        for at in range(local):
            for i in range(len(cuts)):
                dual_copy(at, i).wait()


def fused(gathered, base_weight, keep_mask, dual_start, topk):
    local, tall, width = base_weight.shape
    chunk = 512
    tokens = gathered[0].shape[0]
    slots = min(-(-tokens // ROWS_BLOCK) * MOST, tokens)
    slots = -(-slots // LANES) * LANES
    whole = pl.BlockSpec(memory_space=pltpu.VMEM)
    anywhere = pl.BlockSpec(memory_space=pl.ANY)
    out = jax.ShapeDtypeStruct(dual_start.shape, F32)
    macs = local * slots * width * (4 * tall + tokens)
    scoped = 4 * tall * width + 4 * slots * (width + tokens) + SPARE * MIB
    held = [pltpu.with_memory_space_constraint(x, pltpu.VMEM) for x in (*gathered, base_weight, dual_start)]
    outs = pl.pallas_call(
        functools.partial(fused_kernel, chunk, topk, len(gathered)),
        grid=(local,),
        in_specs=[whole] * (len(held) + 1),
        out_specs=[anywhere, anywhere, whole],
        out_shape=[out, out, pltpu.VMEM(dual_start.shape, F32)],
        input_output_aliases={len(held) - 1: 2},
        scratch_shapes=[
            pltpu.VMEM((slots, width), BF16),
            pltpu.VMEM((width, slots), BF16),
            pltpu.VMEM((tall, width), F32),
            pltpu.VMEM((local, tokens), F32),
            pltpu.VMEM((local, tokens), F32),
            pltpu.VMEM((local, keep_mask.shape[1], width), F32),
            pltpu.SemaphoreType.DMA((width // chunk,)),
            pltpu.SemaphoreType.DMA((local, width // chunk)),
        ],
        compiler_params=pltpu.CompilerParams(vmem_limit_bytes=scoped, dimension_semantics=("arbitrary",)),
        cost_estimate=pl.CostEstimate(flops=2 * macs, bytes_accessed=8 * base_weight.size, transcendentals=0),
    )(*held, keep_mask)
    return outs[0], outs[1]


def plain(gathered, base_weight, keep_mask, dual, topk):
    local, _, width = base_weight.shape
    part = width // len(gathered)
    routes = gathered[0][:, part : part + topk].astype(jnp.int32)
    rows = jnp.concatenate([piece[:, :part] for piece in gathered], axis=1)
    tokens = rows.shape[0]
    slots = min(-(-tokens // ROWS_BLOCK) * MOST, tokens)
    labels = lax.axis_index("exp") * local + jnp.arange(local, dtype=jnp.int32)
    hits = jnp.any(routes[:, :, None] == labels, axis=1)
    rank = jnp.cumsum(hits.astype(jnp.int32), axis=0) - 1
    taken = hits[:, :, None] & (rank[:, :, None] == jnp.arange(slots, dtype=jnp.int32))
    picked = jnp.einsum("rls,rd->lsd", taken.astype(BF16), rows, preferred_element_type=F32).astype(BF16)
    rate = (step_rate / jnp.sum(hits.astype(F32), axis=0))[:, None, None]
    mask = jnp.repeat(jnp.repeat(keep_mask.astype(F32), BLOCK, 1), BLOCK, 2)
    base = base_weight.astype(F32)
    weight = zed = mask * base
    for _ in range(ITERS):
        delta = (weight - base).astype(BF16)
        resid = jnp.einsum("lnd,lcd->lcn", picked, delta, preferred_element_type=F32).astype(BF16)
        grad = jnp.einsum("lcn,lnd->lcd", resid, picked, preferred_element_type=F32)
        weight = weight - rate * grad - step_rate * (weight - zed + dual)
        zed = mask * (weight + dual)
        dual = dual + weight - zed
    return weight, dual


def spread(own):
    n_tok, n_exp = lax.axis_size("tok"), lax.axis_size("exp")
    top = n_exp.bit_length() - 1
    assert 1 << top == n_exp

    def swap(piece, bit):
        return lax.ppermute(piece, "exp", [(i, i ^ (1 << bit)) for i in range(n_exp)])

    column = [own]
    for shift in range(1, n_tok):
        column.append(lax.ppermute(own, "tok", [(i, (i + shift) % n_tok) for i in range(n_tok)]))
    pieces = {0: jnp.concatenate(column, axis=0)}
    if top == 3:
        one, two = swap(pieces[0], 1), swap(pieces[0], 2)
        middle = own.shape[1] // 2 // LANES * LANES
        far = jnp.concatenate([swap(one[:, :middle], 2), swap(two[:, middle:], 1)], axis=1)
        pieces.update({2: one, 4: two, 6: far})
    else:
        for bit in range(1, top):
            pieces.update({at ^ (1 << bit): swap(piece, bit) for at, piece in pieces.items()})
    pieces.update({at ^ 1: swap(piece, 0) for at, piece in pieces.items()})
    first = [pieces[i] for i in range(n_exp) if i > 1 and i.bit_count() == 1]
    return jnp.concatenate([pieces[i] for i in range(n_exp)], axis=0), first


def on_device(x_rows, routes, base_weight, keep_mask, dual_start):
    local, hidden, width = base_weight.shape
    topk = routes.shape[1]
    halves = 2
    part = width // halves
    named = jnp.pad(routes.astype(BF16), ((0, 0), (0, LANES - topk)))
    sent = [x_rows[:, h * part : (h + 1) * part] for h in range(halves)]
    sent[0] = jnp.concatenate([sent[0], named], axis=1)
    with jax.named_scope("exchange_rows"):
        gathered, marks = zip(*[spread(own) for own in sent])
    if 2 * gathered[0].shape[0] * width > 16 * MIB:
        return plain(gathered, base_weight, keep_mask, dual_start, topk)
    with jax.named_scope("load_weights"):
        base_weight, dual_start = load(marks[-1], base_weight, dual_start)
    with jax.named_scope("fused_iterations"):
        return fused(gathered, base_weight, keep_mask, dual_start, topk)


def solution(mesh):
    return jax.shard_map(
        on_device,
        mesh=mesh,
        in_specs=(
            P(("tok", "exp"), None),
            P(("tok", "exp"), None),
            P("exp", "tok", None),
            P("exp", "tok", None),
            P("exp", "tok", None),
        ),
        out_specs=(P("exp", "tok", None), P("exp", "tok", None)),
        check_vma=False,
    )
```

```python
import functools

import jax
import jax.numpy as jnp
from jax import lax
from jax.experimental import pallas as pl
from jax.experimental.pallas import tpu as pltpu
from jax.sharding import PartitionSpec as P

EXPERTS = 32
BLOCK = 64
ROWS_BLOCK = 24
MOST = 7
ITERS = 2
LANES = 128
MIB = 1024 * 1024
SPARE = 6

step_rate = 0.2

F32 = jnp.float32
BF16 = jnp.bfloat16


def dot_nn(a, b):
    return jnp.dot(a, b, preferred_element_type=F32)


def dot_nt(a, b):
    return lax.dot_general(a, b, (((1,), (1,)), ((), ())), preferred_element_type=F32)


def cuts_of(width, chunk):
    return [pl.ds(start, chunk) for start in range(0, width, chunk)]


def load_kernel(n_marks, *refs):
    base_ref, dual_ref, base_out, dual_out, token, sems = refs[n_marks:]
    copies = [
        pltpu.make_async_copy(base_ref, base_out, sems.at[0]),
        pltpu.make_async_copy(dual_ref, dual_out, sems.at[1]),
    ]
    for copy in copies:
        copy.start()
    token[...] = jnp.ones_like(token)
    for copy in copies:
        copy.wait()


def load(marks, base_weight, dual_start):
    anywhere = pl.BlockSpec(memory_space=pl.ANY)
    return pl.pallas_call(
        functools.partial(load_kernel, len(marks)),
        in_specs=[anywhere] * (len(marks) + 2),
        out_specs=[anywhere, anywhere, pl.BlockSpec(memory_space=pltpu.VMEM)],
        out_shape=[pltpu.VMEM(x.shape, x.dtype) for x in (base_weight, dual_start)]
        + [jax.ShapeDtypeStruct(marks[0].shape, BF16)],
        scratch_shapes=[pltpu.SemaphoreType.DMA((2,))],
        compiler_params=pltpu.CompilerParams(vmem_limit_bytes=16 * MIB),
        cost_estimate=pl.CostEstimate(flops=0, bytes_accessed=6 * base_weight.size, transcendentals=0),
    )(*marks, base_weight, dual_start)


def fused_kernel(chunk, topk, halves, *refs):
    gathered = refs[:halves]
    base_ref, _, keep_ref, weight_hbm, dual_hbm, dual, *refs = refs[halves:]
    rows, across, held, rank, hits, mask, weight_sems, dual_sems = refs
    expert = pl.program_id(0)
    tokens = gathered[0].shape[0]
    slots, width = rows.shape
    part_width = width // halves
    local, tall, _ = base_ref.shape
    cuts = cuts_of(width, chunk)
    parts = [slice(start, start + BLOCK) for start in range(0, tall, BLOCK)]

    def weight_copy(at, i):
        return pltpu.make_async_copy(held.at[:, cuts[i]], weight_hbm.at[at, :, cuts[i]], weight_sems.at[i])

    def dual_copy(at, i):
        return pltpu.make_async_copy(dual.at[at, :, cuts[i]], dual_hbm.at[at, :, cuts[i]], dual_sems.at[at, i])

    @pl.when(expert == 0)
    def _():
        named = gathered[0][:, pl.ds(part_width, LANES)].astype(F32).T[:topk, :]
        for own in range(local):
            label = (lax.axis_index("exp") * local + own).astype(F32)
            hits[own : own + 1, :] = jnp.max(jnp.where(named == label, 1.0, 0.0), axis=0, keepdims=True)
        earlier = lax.broadcasted_iota(jnp.int32, (tokens, tokens), 0)
        later = lax.broadcasted_iota(jnp.int32, (tokens, tokens), 1)
        ahead = jnp.where(earlier < later, 1.0, 0.0).astype(BF16)
        rank[...] = dot_nn(hits[...].astype(BF16), ahead)
        count = keep_ref.shape[2]
        at = lax.broadcasted_iota(jnp.int32, (count, width), 0) * BLOCK
        column = lax.broadcasted_iota(jnp.int32, (count, width), 1)
        wide = jnp.where((column >= at) & (column < at + BLOCK), 1.0, 0.0).astype(BF16)
        for own in range(local):
            mask[own] = dot_nn(keep_ref[own].astype(F32).astype(BF16), wide)

    hit = hits[pl.ds(expert, 1), :]
    place = rank[pl.ds(expert, 1), :]
    slot = lax.broadcasted_iota(jnp.int32, (slots, tokens), 0).astype(F32)
    taken = jnp.where((slot == place) & (hit > 0.5), 1.0, 0.0).astype(BF16)
    rate = step_rate / jnp.sum(hit, axis=1, keepdims=True)
    resid = jnp.zeros((tall, slots), F32)
    for cut in cuts:
        half, start = divmod(cut.start, part_width)
        picked = dot_nn(taken, gathered[half][:, pl.ds(start, chunk)])
        rows[:, cut] = picked.astype(BF16)
        across[cut, :] = picked.T.astype(BF16)
        deltas = [
            base_ref[expert, part, cut] * (mask[expert, i : i + 1, cut] - 1.0).astype(BF16) for i, part in enumerate(parts)
        ]
        resid = resid + dot_nn(jnp.concatenate(deltas, axis=0), across[cut, :])
    resid = resid.astype(BF16)

    @pl.when(expert > 0)
    def _():
        for i in range(len(cuts)):
            weight_copy(expert - 1, i).wait()

    after = jnp.zeros((tall, slots), F32)
    for cut in cuts:
        grad = dot_nn(resid, rows[:, cut])
        deltas = []
        for i, part in enumerate(parts):
            base = base_ref[expert, part, cut].astype(F32)
            weight = mask[expert, i : i + 1, cut] * base - step_rate * dual[expert, part, cut] - rate * grad[part, :]
            held[part, cut] = weight
            deltas.append((weight - base).astype(BF16))
        after = after + dot_nn(jnp.concatenate(deltas, axis=0), across[cut, :])
    resid = after.astype(BF16)

    for n, cut in enumerate(cuts):
        grad = dot_nn(resid, rows[:, cut])
        for i, part in enumerate(parts):
            keep = mask[expert, i : i + 1, cut]
            weight = held[part, cut]
            both = weight + dual[expert, part, cut]
            weight = (1.0 - step_rate) * weight - (step_rate - 2.0 * step_rate * keep) * both - rate * grad[part, :]
            held[part, cut] = weight
            dual[expert, part, cut] = (1.0 - keep) * (both + weight)
        weight_copy(expert, n).start()
        dual_copy(expert, n).start()

    @pl.when(expert == local - 1)
    def _():
        for i in range(len(cuts)):
            weight_copy(expert, i).wait()
        for at in range(local):
            for i in range(len(cuts)):
                dual_copy(at, i).wait()


def fused(gathered, base_weight, keep_mask, dual_start, topk):
    local, tall, width = base_weight.shape
    chunk = 512
    tokens = gathered[0].shape[0]
    slots = min(-(-tokens // ROWS_BLOCK) * MOST, tokens)
    slots = -(-slots // LANES) * LANES
    whole = pl.BlockSpec(memory_space=pltpu.VMEM)
    anywhere = pl.BlockSpec(memory_space=pl.ANY)
    out = jax.ShapeDtypeStruct(dual_start.shape, F32)
    macs = local * slots * width * (4 * tall + tokens)
    scoped = 4 * tall * width + 4 * slots * (width + tokens) + SPARE * MIB
    held = [pltpu.with_memory_space_constraint(x, pltpu.VMEM) for x in (*gathered, base_weight, dual_start)]
    outs = pl.pallas_call(
        functools.partial(fused_kernel, chunk, topk, len(gathered)),
        grid=(local,),
        in_specs=[whole] * (len(held) + 1),
        out_specs=[anywhere, anywhere, whole],
        out_shape=[out, out, pltpu.VMEM(dual_start.shape, F32)],
        input_output_aliases={len(held) - 1: 2},
        scratch_shapes=[
            pltpu.VMEM((slots, width), BF16),
            pltpu.VMEM((width, slots), BF16),
            pltpu.VMEM((tall, width), F32),
            pltpu.VMEM((local, tokens), F32),
            pltpu.VMEM((local, tokens), F32),
            pltpu.VMEM((local, keep_mask.shape[1], width), F32),
            pltpu.SemaphoreType.DMA((width // chunk,)),
            pltpu.SemaphoreType.DMA((local, width // chunk)),
        ],
        compiler_params=pltpu.CompilerParams(vmem_limit_bytes=scoped, dimension_semantics=("arbitrary",)),
        cost_estimate=pl.CostEstimate(flops=2 * macs, bytes_accessed=8 * base_weight.size, transcendentals=0),
    )(*held, keep_mask)
    return outs[0], outs[1]


def plain(gathered, base_weight, keep_mask, dual, topk):
    local, _, width = base_weight.shape
    part = width // len(gathered)
    routes = gathered[0][:, part : part + topk].astype(jnp.int32)
    rows = jnp.concatenate([piece[:, :part] for piece in gathered], axis=1)
    tokens = rows.shape[0]
    slots = min(-(-tokens // ROWS_BLOCK) * MOST, tokens)
    labels = lax.axis_index("exp") * local + jnp.arange(local, dtype=jnp.int32)
    hits = jnp.any(routes[:, :, None] == labels, axis=1)
    rank = jnp.cumsum(hits.astype(jnp.int32), axis=0) - 1
    taken = hits[:, :, None] & (rank[:, :, None] == jnp.arange(slots, dtype=jnp.int32))
    picked = jnp.einsum("rls,rd->lsd", taken.astype(BF16), rows, preferred_element_type=F32).astype(BF16)
    rate = (step_rate / jnp.sum(hits.astype(F32), axis=0))[:, None, None]
    mask = jnp.repeat(jnp.repeat(keep_mask.astype(F32), BLOCK, 1), BLOCK, 2)
    base = base_weight.astype(F32)
    weight = zed = mask * base
    for _ in range(ITERS):
        delta = (weight - base).astype(BF16)
        resid = jnp.einsum("lnd,lcd->lcn", picked, delta, preferred_element_type=F32).astype(BF16)
        grad = jnp.einsum("lcn,lnd->lcd", resid, picked, preferred_element_type=F32)
        weight = weight - rate * grad - step_rate * (weight - zed + dual)
        zed = mask * (weight + dual)
        dual = dual + weight - zed
    return weight, dual


def after(ones, array):
    return array * ones[: array.shape[0], : array.shape[1]]


def swap(piece, bit):
    n = lax.axis_size("exp")
    return lax.ppermute(piece, "exp", [(i, i ^ (1 << bit)) for i in range(n)])


def column_rows(own):
    n = lax.axis_size("tok")
    column = [own]
    for shift in range(1, n):
        column.append(lax.ppermute(own, "tok", [(i, (i + shift) % n) for i in range(n)]))
    return jnp.concatenate(column, axis=0)


def on_device(x_rows, routes, base_weight, keep_mask, dual_start):
    local, hidden, width = base_weight.shape
    topk = routes.shape[1]
    n_exp = lax.axis_size("exp")
    top = n_exp.bit_length() - 1
    assert 1 << top == n_exp
    named = jnp.pad(routes.astype(BF16), ((0, 0), (0, LANES - topk)))
    with jax.named_scope("exchange_rows"):
        mine = column_rows(jnp.concatenate([x_rows, named], axis=1))
    if top != 3 or 2 * n_exp * mine.shape[0] * width > 16 * MIB:
        pieces = {0: mine}
        for bit in [*range(1, top), 0]:
            pieces.update({at ^ (1 << bit): swap(piece, bit) for at, piece in pieces.items()})
        gathered = jnp.concatenate([pieces[i] for i in range(n_exp)], axis=0)
        return plain([gathered], base_weight, keep_mask, dual_start, topk)
    with jax.named_scope("load_weights"):
        base_weight, dual_start, token = load([mine], base_weight, dual_start)
    with jax.named_scope("exchange_rows"):
        one, two = swap(mine, 1), swap(mine, 2)
        middle = mine.shape[1] // 2 // LANES * LANES
        far = [swap(after(token, one[:, :middle]), 2), swap(after(token, two[:, middle:]), 1)]
        pieces = [mine, one, two, jnp.concatenate(far, axis=1)]
        pieces += [swap(piece, 0) for piece in pieces]
    gathered = [jnp.concatenate(pieces, axis=0)]
    with jax.named_scope("fused_iterations"):
        return fused(gathered, base_weight, keep_mask, dual_start, topk)


def solution(mesh):
    return jax.shard_map(
        on_device,
        mesh=mesh,
        in_specs=(
            P(("tok", "exp"), None),
            P(("tok", "exp"), None),
            P("exp", "tok", None),
            P("exp", "tok", None),
            P("exp", "tok", None),
        ),
        out_specs=(P("exp", "tok", None), P("exp", "tok", None)),
        check_vma=False,
    )
```

```python
import functools

import jax
import jax.numpy as jnp
from jax import lax
from jax.experimental import pallas as pl
from jax.experimental.pallas import tpu as pltpu
from jax.sharding import PartitionSpec as P

EXPERTS = 32
BLOCK = 64
ROWS_BLOCK = 24
MOST = 7
ITERS = 2
LANES = 128
MIB = 1024 * 1024
SPARE = 10

step_rate = 0.2

F32 = jnp.float32
BF16 = jnp.bfloat16


def dot_nn(a, b):
    return jnp.dot(a, b, preferred_element_type=F32)


def dot_nt(a, b):
    return lax.dot_general(a, b, (((1,), (1,)), ((), ())), preferred_element_type=F32)


def cuts_of(width, chunk):
    return [pl.ds(start, chunk) for start in range(0, width, chunk)]


def load_kernel(n_marks, *refs):
    source, held, token, sem = refs[n_marks:]
    copy = pltpu.make_async_copy(source, held, sem)
    copy.start()
    token[...] = jnp.ones_like(token)
    copy.wait()


def load(marks, array, scoped):
    anywhere = pl.BlockSpec(memory_space=pl.ANY)
    size = array.size * array.dtype.itemsize
    return pl.pallas_call(
        functools.partial(load_kernel, len(marks)),
        in_specs=[anywhere] * (len(marks) + 1),
        out_specs=[anywhere, pl.BlockSpec(memory_space=pltpu.VMEM)],
        out_shape=[pltpu.VMEM(array.shape, array.dtype), jax.ShapeDtypeStruct(marks[0].shape, BF16)],
        scratch_shapes=[pltpu.SemaphoreType.DMA],
        compiler_params=pltpu.CompilerParams(vmem_limit_bytes=scoped),
        cost_estimate=pl.CostEstimate(flops=0, bytes_accessed=size, transcendentals=0),
    )(*marks, array)


def fused_kernel(chunk, topk, halves, block_rows, *refs):
    gathered = refs[:halves]
    base_hbm, _, keep_ref, weight_hbm, dual_hbm, dual, *refs = refs[halves:]
    base_held, rows, across, held, mask, counts, base_sem, weight_sems, dual_sems = refs
    expert = pl.program_id(0)
    tokens = gathered[0].shape[0]
    local, slots, width = rows.shape
    tall = held.shape[0]
    part_width = width // halves
    cuts = cuts_of(width, chunk)
    parts = [slice(start, start + BLOCK) for start in range(0, tall, BLOCK)]
    per = slots // (tokens // block_rows)
    lanes = local * per

    def base_copy(at):
        return pltpu.make_async_copy(base_hbm.at[at], base_held, base_sem)

    def weight_copy(at, i):
        return pltpu.make_async_copy(held.at[:, cuts[i]], weight_hbm.at[at, :, cuts[i]], weight_sems.at[i])

    def dual_copy(at, i):
        return pltpu.make_async_copy(dual.at[at, :, cuts[i]], dual_hbm.at[at, :, cuts[i]], dual_sems.at[at, i])

    @pl.when(expert == 0)
    def _():
        base_copy(0).start()
        lane = lax.broadcasted_iota(jnp.int32, (block_rows, lanes), 1)
        which = sum(jnp.where(lane >= per * own, 1, 0) for own in range(1, local))
        label = (lax.axis_index("exp") * local + which).astype(F32)
        slot = (lane - which * per).astype(F32)
        later = lax.broadcasted_iota(jnp.int32, (block_rows, block_rows), 0)
        earlier = lax.broadcasted_iota(jnp.int32, (block_rows, block_rows), 1)
        ahead = jnp.where(earlier < later, 1.0, 0.0).astype(BF16)

        def pack(p, total):
            block = pl.ds(pl.multiple_of(p * block_rows, 16), block_rows)
            named = gathered[0][block, pl.ds(part_width, LANES)].astype(F32)
            hit = jnp.zeros((block_rows, lanes), F32)
            for k in range(topk):
                hit = jnp.where(named[:, k : k + 1] == label, 1.0, hit)
            taken = jnp.where(dot_nn(ahead, hit.astype(BF16)) == slot, hit, 0.0)
            spare = jnp.zeros((-block_rows % LANES, lanes), F32)
            taken = jnp.concatenate([taken, spare], axis=0).T[:, :block_rows].astype(BF16)
            for cut in cuts:
                half, start = divmod(cut.start, part_width)
                picked = dot_nn(taken, gathered[half][block, pl.ds(start, chunk)]).astype(BF16)
                for own in range(local):
                    rows[own, pl.ds(pl.multiple_of(p * per, 16), per), cut] = picked[own * per : (own + 1) * per, :]
            return total + jnp.sum(hit, axis=0, keepdims=True)

        counts[...] = lax.fori_loop(0, tokens // block_rows, pack, jnp.zeros((1, lanes), F32))
        count = keep_ref.shape[2]
        at = lax.broadcasted_iota(jnp.int32, (count, width), 0) * BLOCK
        column = lax.broadcasted_iota(jnp.int32, (count, width), 1)
        wide = jnp.where((column >= at) & (column < at + BLOCK), 1.0, 0.0).astype(BF16)
        for own in range(local):
            mask[own] = dot_nn(keep_ref[own].astype(F32).astype(BF16), wide)

    base_copy(expert).wait()
    mine = lax.broadcasted_iota(jnp.int32, (1, lanes), 1) == expert * per
    rate = step_rate / jnp.sum(jnp.where(mine, counts[...], 0.0), axis=1, keepdims=True)

    resid = jnp.zeros((tall, slots), F32)
    for cut in cuts:
        across[cut, :] = rows[expert, :, cut].T
        deltas = [
            base_held[part, cut] * (mask[expert, i : i + 1, cut] - 1.0).astype(BF16) for i, part in enumerate(parts)
        ]
        resid = resid + dot_nn(jnp.concatenate(deltas, axis=0), across[cut, :])
    resid = resid.astype(BF16)

    @pl.when(expert > 0)
    def _():
        for i in range(len(cuts)):
            weight_copy(expert - 1, i).wait()

    after = jnp.zeros((tall, slots), F32)
    for cut in cuts:
        grad = dot_nn(resid, rows[expert, :, cut])
        deltas = []
        for i, part in enumerate(parts):
            base = base_held[part, cut].astype(F32)
            weight = mask[expert, i : i + 1, cut] * base - step_rate * dual[expert, part, cut] - rate * grad[part, :]
            held[part, cut] = weight
            deltas.append((weight - base).astype(BF16))
        after = after + dot_nn(jnp.concatenate(deltas, axis=0), across[cut, :])
    resid = after.astype(BF16)

    @pl.when(expert < local - 1)
    def _():
        base_copy(expert + 1).start()

    for n, cut in enumerate(cuts):
        grad = dot_nn(resid, rows[expert, :, cut])
        for i, part in enumerate(parts):
            keep = mask[expert, i : i + 1, cut]
            weight = held[part, cut]
            both = weight + dual[expert, part, cut]
            weight = (1.0 - step_rate) * weight - (step_rate - 2.0 * step_rate * keep) * both - rate * grad[part, :]
            held[part, cut] = weight
            dual[expert, part, cut] = (1.0 - keep) * (both + weight)
        weight_copy(expert, n).start()
        dual_copy(expert, n).start()

    @pl.when(expert == local - 1)
    def _():
        for i in range(len(cuts)):
            weight_copy(expert, i).wait()
        for at in range(local):
            for i in range(len(cuts)):
                dual_copy(at, i).wait()


def fused(gathered, base_weight, keep_mask, dual_start, topk, per, scoped):
    local, tall, width = base_weight.shape
    chunk = 512
    block_rows = gathered[0].shape[0] // lax.axis_size("exp")
    slots = lax.axis_size("exp") * per
    whole = pl.BlockSpec(memory_space=pltpu.VMEM)
    anywhere = pl.BlockSpec(memory_space=pl.ANY)
    out = jax.ShapeDtypeStruct(dual_start.shape, F32)
    macs = local * slots * width * (4 * tall + block_rows)
    held = [pltpu.with_memory_space_constraint(x, pltpu.VMEM) for x in (*gathered, dual_start)]
    operands = [*held[:-1], base_weight, held[-1], keep_mask]
    outs = pl.pallas_call(
        functools.partial(fused_kernel, chunk, topk, len(gathered), block_rows),
        grid=(local,),
        in_specs=[whole] * len(gathered) + [anywhere, whole, whole],
        out_specs=[anywhere, anywhere, whole],
        out_shape=[out, out, pltpu.VMEM(dual_start.shape, F32)],
        input_output_aliases={len(operands) - 2: 2},
        scratch_shapes=[
            pltpu.VMEM((tall, width), BF16),
            pltpu.VMEM((local, slots, width), BF16),
            pltpu.VMEM((width, slots), BF16),
            pltpu.VMEM((tall, width), F32),
            pltpu.VMEM((local, keep_mask.shape[1], width), F32),
            pltpu.VMEM((1, local * per), F32),
            pltpu.SemaphoreType.DMA,
            pltpu.SemaphoreType.DMA((width // chunk,)),
            pltpu.SemaphoreType.DMA((local, width // chunk)),
        ],
        compiler_params=pltpu.CompilerParams(vmem_limit_bytes=scoped, dimension_semantics=("arbitrary",)),
        cost_estimate=pl.CostEstimate(flops=2 * macs, bytes_accessed=8 * base_weight.size, transcendentals=0),
    )(*operands)
    return outs[0], outs[1]


def plain(gathered, base_weight, keep_mask, dual, topk):
    local, _, width = base_weight.shape
    part = width // len(gathered)
    routes = gathered[0][:, part : part + topk].astype(jnp.int32)
    rows = jnp.concatenate([piece[:, :part] for piece in gathered], axis=1)
    tokens = rows.shape[0]
    slots = min(-(-tokens // ROWS_BLOCK) * MOST, tokens)
    labels = lax.axis_index("exp") * local + jnp.arange(local, dtype=jnp.int32)
    hits = jnp.any(routes[:, :, None] == labels, axis=1)
    rank = jnp.cumsum(hits.astype(jnp.int32), axis=0) - 1
    taken = hits[:, :, None] & (rank[:, :, None] == jnp.arange(slots, dtype=jnp.int32))
    picked = jnp.einsum("rls,rd->lsd", taken.astype(BF16), rows, preferred_element_type=F32).astype(BF16)
    rate = (step_rate / jnp.sum(hits.astype(F32), axis=0))[:, None, None]
    mask = jnp.repeat(jnp.repeat(keep_mask.astype(F32), BLOCK, 1), BLOCK, 2)
    base = base_weight.astype(F32)
    weight = zed = mask * base
    for _ in range(ITERS):
        delta = (weight - base).astype(BF16)
        resid = jnp.einsum("lnd,lcd->lcn", picked, delta, preferred_element_type=F32).astype(BF16)
        grad = jnp.einsum("lcn,lnd->lcd", resid, picked, preferred_element_type=F32)
        weight = weight - rate * grad - step_rate * (weight - zed + dual)
        zed = mask * (weight + dual)
        dual = dual + weight - zed
    return weight, dual


def after(ones, array):
    return array * ones[: array.shape[0], : array.shape[1]]


def swap(piece, bit):
    n = lax.axis_size("exp")
    return lax.ppermute(piece, "exp", [(i, i ^ (1 << bit)) for i in range(n)])


def column_rows(own):
    n = lax.axis_size("tok")
    column = [own]
    for shift in range(1, n):
        column.append(lax.ppermute(own, "tok", [(i, (i + shift) % n) for i in range(n)]))
    return jnp.concatenate(column, axis=0)


def on_device(x_rows, routes, base_weight, keep_mask, dual_start):
    local, hidden, width = base_weight.shape
    topk = routes.shape[1]
    n_exp = lax.axis_size("exp")
    top = n_exp.bit_length() - 1
    assert 1 << top == n_exp
    halves = 2
    part = width // halves
    named = jnp.pad(routes.astype(BF16), ((0, 0), (0, LANES - topk)))
    sent = [x_rows[:, h * part : (h + 1) * part] for h in range(halves)]
    sent[0] = jnp.concatenate([sent[0], named], axis=1)
    with jax.named_scope("exchange_rows"):
        mine = [column_rows(own) for own in sent]
    if top != 3 or 2 * n_exp * mine[0].shape[0] * width > 16 * MIB:
        gathered = []
        for own in mine:
            pieces = {0: own}
            for bit in [*range(1, top), 0]:
                pieces.update({at ^ (1 << bit): swap(piece, bit) for at, piece in pieces.items()})
            gathered.append(jnp.concatenate([pieces[i] for i in range(n_exp)], axis=0))
        return plain(gathered, base_weight, keep_mask, dual_start, topk)
    per = -(-(mine[0].shape[0] // ROWS_BLOCK) * MOST // 16) * 16
    scoped = 6 * hidden * width + 2 * (local + 1) * n_exp * per * width + SPARE * MIB
    with jax.named_scope("load_duals"):
        dual_start, token = load(mine, dual_start, scoped)
    gathered = []
    with jax.named_scope("exchange_rows"):
        for own in mine:
            one, two = swap(own, 1), swap(own, 2)
            middle = own.shape[1] // 2 // LANES * LANES
            far = [swap(after(token, one[:, :middle]), 2), swap(after(token, two[:, middle:]), 1)]
            pieces = [own, one, two, jnp.concatenate(far, axis=1)]
            gathered.append(jnp.concatenate(pieces + [swap(piece, 0) for piece in pieces], axis=0))
    with jax.named_scope("fused_iterations"):
        return fused(gathered, base_weight, keep_mask, dual_start, topk, per, scoped)


def solution(mesh):
    return jax.shard_map(
        on_device,
        mesh=mesh,
        in_specs=(
            P(("tok", "exp"), None),
            P(("tok", "exp"), None),
            P("exp", "tok", None),
            P("exp", "tok", None),
            P("exp", "tok", None),
        ),
        out_specs=(P("exp", "tok", None), P("exp", "tok", None)),
        check_vma=False,
    )
```

```python
import functools

import jax
import jax.numpy as jnp
from jax import lax
from jax.experimental import pallas as pl
from jax.experimental.pallas import tpu as pltpu
from jax.sharding import PartitionSpec as P

EXPERTS = 32
BLOCK = 64
ROWS_BLOCK = 24
MOST = 7
ITERS = 2
LANES = 128
MIB = 1024 * 1024
SPARE = 6

step_rate = 0.2

F32 = jnp.float32
BF16 = jnp.bfloat16


def dot_nn(a, b):
    return jnp.dot(a, b, preferred_element_type=F32)


def dot_nt(a, b):
    return lax.dot_general(a, b, (((1,), (1,)), ((), ())), preferred_element_type=F32)


def cuts_of(width, chunk):
    return [pl.ds(start, chunk) for start in range(0, width, chunk)]


def load_kernel(n_marks, *refs):
    base_ref, dual_ref, base_out, dual_out, token, sems = refs[n_marks:]
    copies = [
        pltpu.make_async_copy(base_ref, base_out, sems.at[0]),
        pltpu.make_async_copy(dual_ref, dual_out, sems.at[1]),
    ]
    for copy in copies:
        copy.start()
    token[...] = jnp.ones_like(token)
    for copy in copies:
        copy.wait()


def load(marks, base_weight, dual_start):
    anywhere = pl.BlockSpec(memory_space=pl.ANY)
    return pl.pallas_call(
        functools.partial(load_kernel, len(marks)),
        in_specs=[anywhere] * (len(marks) + 2),
        out_specs=[anywhere, anywhere, pl.BlockSpec(memory_space=pltpu.VMEM)],
        out_shape=[pltpu.VMEM(x.shape, x.dtype) for x in (base_weight, dual_start)]
        + [jax.ShapeDtypeStruct(marks[0].shape, BF16)],
        scratch_shapes=[pltpu.SemaphoreType.DMA((2,))],
        compiler_params=pltpu.CompilerParams(vmem_limit_bytes=16 * MIB),
        cost_estimate=pl.CostEstimate(flops=0, bytes_accessed=6 * base_weight.size, transcendentals=0),
    )(*marks, base_weight, dual_start)


def fused_kernel(chunk, topk, halves, *refs):
    gathered = refs[:halves]
    base_ref, _, keep_ref, weight_hbm, dual_hbm, dual, *refs = refs[halves:]
    rows, held, rank, hits, mask, weight_sems, dual_sems = refs
    expert = pl.program_id(0)
    tokens = gathered[0].shape[0]
    slots, width = rows.shape
    part_width = width // halves
    local, tall, _ = base_ref.shape
    cuts = cuts_of(width, chunk)
    parts = [slice(start, start + BLOCK) for start in range(0, tall, BLOCK)]

    def weight_copy(at, i):
        return pltpu.make_async_copy(held.at[:, cuts[i]], weight_hbm.at[at, :, cuts[i]], weight_sems.at[i])

    def dual_copy(at, i):
        return pltpu.make_async_copy(dual.at[at, :, cuts[i]], dual_hbm.at[at, :, cuts[i]], dual_sems.at[at, i])

    @pl.when(expert == 0)
    def _():
        named = gathered[0][:, pl.ds(part_width, LANES)].astype(F32).T[:topk, :]
        for own in range(local):
            label = (lax.axis_index("exp") * local + own).astype(F32)
            hits[own : own + 1, :] = jnp.max(jnp.where(named == label, 1.0, 0.0), axis=0, keepdims=True)
        earlier = lax.broadcasted_iota(jnp.int32, (tokens, tokens), 0)
        later = lax.broadcasted_iota(jnp.int32, (tokens, tokens), 1)
        ahead = jnp.where(earlier < later, 1.0, 0.0).astype(BF16)
        rank[...] = dot_nn(hits[...].astype(BF16), ahead)
        count = keep_ref.shape[2]
        at = lax.broadcasted_iota(jnp.int32, (count, width), 0) * BLOCK
        column = lax.broadcasted_iota(jnp.int32, (count, width), 1)
        wide = jnp.where((column >= at) & (column < at + BLOCK), 1.0, 0.0).astype(BF16)
        for own in range(local):
            mask[own] = dot_nn(keep_ref[own].astype(F32).astype(BF16), wide)

    hit = hits[pl.ds(expert, 1), :]
    place = rank[pl.ds(expert, 1), :]
    slot = lax.broadcasted_iota(jnp.int32, (slots, tokens), 0).astype(F32)
    taken = jnp.where((slot == place) & (hit > 0.5), 1.0, 0.0).astype(BF16)
    rate = step_rate / jnp.sum(hit, axis=1, keepdims=True)
    resid = jnp.zeros((tall, slots), F32)
    for cut in cuts:
        half, start = divmod(cut.start, part_width)
        rows[:, cut] = dot_nn(taken, gathered[half][:, pl.ds(start, chunk)]).astype(BF16)
        deltas = [
            base_ref[expert, part, cut] * (mask[expert, i : i + 1, cut] - 1.0).astype(BF16) for i, part in enumerate(parts)
        ]
        resid = resid + dot_nt(jnp.concatenate(deltas, axis=0), rows[:, cut])
    resid = resid.astype(BF16)

    @pl.when(expert > 0)
    def _():
        for i in range(len(cuts)):
            weight_copy(expert - 1, i).wait()

    after = jnp.zeros((tall, slots), F32)
    for cut in cuts:
        grad = dot_nn(resid, rows[:, cut])
        deltas = []
        for i, part in enumerate(parts):
            base = base_ref[expert, part, cut].astype(F32)
            weight = mask[expert, i : i + 1, cut] * base - step_rate * dual[expert, part, cut] - rate * grad[part, :]
            held[part, cut] = weight
            deltas.append((weight - base).astype(BF16))
        after = after + dot_nt(jnp.concatenate(deltas, axis=0), rows[:, cut])
    resid = after.astype(BF16)

    for n, cut in enumerate(cuts):
        grad = dot_nn(resid, rows[:, cut])
        for i, part in enumerate(parts):
            keep = mask[expert, i : i + 1, cut]
            weight = held[part, cut]
            both = weight + dual[expert, part, cut]
            weight = (1.0 - step_rate) * weight - (step_rate - 2.0 * step_rate * keep) * both - rate * grad[part, :]
            held[part, cut] = weight
            dual[expert, part, cut] = (1.0 - keep) * (both + weight)
        weight_copy(expert, n).start()
        dual_copy(expert, n).start()

    @pl.when(expert == local - 1)
    def _():
        for i in range(len(cuts)):
            weight_copy(expert, i).wait()
        for at in range(local):
            for i in range(len(cuts)):
                dual_copy(at, i).wait()


def fused(gathered, base_weight, keep_mask, dual_start, topk):
    local, tall, width = base_weight.shape
    chunk = 512
    tokens = gathered[0].shape[0]
    slots = min(-(-tokens // ROWS_BLOCK) * MOST, tokens)
    slots = -(-slots // LANES) * LANES
    whole = pl.BlockSpec(memory_space=pltpu.VMEM)
    anywhere = pl.BlockSpec(memory_space=pl.ANY)
    out = jax.ShapeDtypeStruct(dual_start.shape, F32)
    macs = local * slots * width * (4 * tall + tokens)
    scoped = 4 * tall * width + 2 * slots * (width + 2 * tokens) + SPARE * MIB
    held = [pltpu.with_memory_space_constraint(x, pltpu.VMEM) for x in (*gathered, base_weight, dual_start)]
    outs = pl.pallas_call(
        functools.partial(fused_kernel, chunk, topk, len(gathered)),
        grid=(local,),
        in_specs=[whole] * (len(held) + 1),
        out_specs=[anywhere, anywhere, whole],
        out_shape=[out, out, pltpu.VMEM(dual_start.shape, F32)],
        input_output_aliases={len(held) - 1: 2},
        scratch_shapes=[
            pltpu.VMEM((slots, width), BF16),
            pltpu.VMEM((tall, width), F32),
            pltpu.VMEM((local, tokens), F32),
            pltpu.VMEM((local, tokens), F32),
            pltpu.VMEM((local, keep_mask.shape[1], width), F32),
            pltpu.SemaphoreType.DMA((width // chunk,)),
            pltpu.SemaphoreType.DMA((local, width // chunk)),
        ],
        compiler_params=pltpu.CompilerParams(vmem_limit_bytes=scoped, dimension_semantics=("arbitrary",)),
        cost_estimate=pl.CostEstimate(flops=2 * macs, bytes_accessed=8 * base_weight.size, transcendentals=0),
    )(*held, keep_mask)
    return outs[0], outs[1]


def plain(gathered, base_weight, keep_mask, dual, topk):
    local, _, width = base_weight.shape
    part = width // len(gathered)
    routes = gathered[0][:, part : part + topk].astype(jnp.int32)
    rows = jnp.concatenate([piece[:, :part] for piece in gathered], axis=1)
    tokens = rows.shape[0]
    slots = min(-(-tokens // ROWS_BLOCK) * MOST, tokens)
    labels = lax.axis_index("exp") * local + jnp.arange(local, dtype=jnp.int32)
    hits = jnp.any(routes[:, :, None] == labels, axis=1)
    rank = jnp.cumsum(hits.astype(jnp.int32), axis=0) - 1
    taken = hits[:, :, None] & (rank[:, :, None] == jnp.arange(slots, dtype=jnp.int32))
    picked = jnp.einsum("rls,rd->lsd", taken.astype(BF16), rows, preferred_element_type=F32).astype(BF16)
    rate = (step_rate / jnp.sum(hits.astype(F32), axis=0))[:, None, None]
    mask = jnp.repeat(jnp.repeat(keep_mask.astype(F32), BLOCK, 1), BLOCK, 2)
    base = base_weight.astype(F32)
    weight = zed = mask * base
    for _ in range(ITERS):
        delta = (weight - base).astype(BF16)
        resid = jnp.einsum("lnd,lcd->lcn", picked, delta, preferred_element_type=F32).astype(BF16)
        grad = jnp.einsum("lcn,lnd->lcd", resid, picked, preferred_element_type=F32)
        weight = weight - rate * grad - step_rate * (weight - zed + dual)
        zed = mask * (weight + dual)
        dual = dual + weight - zed
    return weight, dual


def after(ones, array):
    return array * ones[: array.shape[0], : array.shape[1]]


def swap(piece, bit):
    n = lax.axis_size("exp")
    return lax.ppermute(piece, "exp", [(i, i ^ (1 << bit)) for i in range(n)])


def column_rows(own):
    n = lax.axis_size("tok")
    column = [own]
    for shift in range(1, n):
        column.append(lax.ppermute(own, "tok", [(i, (i + shift) % n) for i in range(n)]))
    return jnp.concatenate(column, axis=0)


def on_device(x_rows, routes, base_weight, keep_mask, dual_start):
    local, hidden, width = base_weight.shape
    topk = routes.shape[1]
    n_exp = lax.axis_size("exp")
    top = n_exp.bit_length() - 1
    assert 1 << top == n_exp
    halves = 2
    part = width // halves
    named = jnp.pad(routes.astype(BF16), ((0, 0), (0, LANES - topk)))
    sent = [x_rows[:, h * part : (h + 1) * part] for h in range(halves)]
    sent[0] = jnp.concatenate([sent[0], named], axis=1)
    with jax.named_scope("exchange_rows"):
        mine = [column_rows(own) for own in sent]
    if top != 3 or 2 * n_exp * mine[0].shape[0] * width > 16 * MIB:
        gathered = []
        for own in mine:
            pieces = {0: own}
            for bit in [*range(1, top), 0]:
                pieces.update({at ^ (1 << bit): swap(piece, bit) for at, piece in pieces.items()})
            gathered.append(jnp.concatenate([pieces[i] for i in range(n_exp)], axis=0))
        return plain(gathered, base_weight, keep_mask, dual_start, topk)
    with jax.named_scope("load_weights"):
        base_weight, dual_start, token = load(mine, base_weight, dual_start)
    gathered = []
    with jax.named_scope("exchange_rows"):
        for own in mine:
            one, two = swap(own, 1), swap(own, 2)
            middle = own.shape[1] // 2 // LANES * LANES
            far = [swap(after(token, one[:, :middle]), 2), swap(after(token, two[:, middle:]), 1)]
            pieces = [own, one, two, jnp.concatenate(far, axis=1)]
            others = [swap(piece, 0) for piece in (after(token, own), *pieces[1:])]
            gathered.append(jnp.concatenate(pieces + others, axis=0))
    with jax.named_scope("fused_iterations"):
        return fused(gathered, base_weight, keep_mask, dual_start, topk)


def solution(mesh):
    return jax.shard_map(
        on_device,
        mesh=mesh,
        in_specs=(
            P(("tok", "exp"), None),
            P(("tok", "exp"), None),
            P("exp", "tok", None),
            P("exp", "tok", None),
            P("exp", "tok", None),
        ),
        out_specs=(P("exp", "tok", None), P("exp", "tok", None)),
        check_vma=False,
    )
```

```python
import functools

import jax
import jax.numpy as jnp
from jax import lax
from jax.experimental import pallas as pl
from jax.experimental.pallas import tpu as pltpu
from jax.sharding import PartitionSpec as P

EXPERTS = 32
BLOCK = 64
ROWS_BLOCK = 24
MOST = 7
ITERS = 2
LANES = 128
MIB = 1024 * 1024
SPARE = 6

step_rate = 0.2

F32 = jnp.float32
BF16 = jnp.bfloat16


def dot_nn(a, b):
    return jnp.dot(a, b, preferred_element_type=F32)


def dot_nt(a, b):
    return lax.dot_general(a, b, (((1,), (1,)), ((), ())), preferred_element_type=F32)


def cuts_of(width, chunk):
    return [pl.ds(start, chunk) for start in range(0, width, chunk)]


def load_kernel(n_marks, *refs):
    base_ref, dual_ref, base_out, dual_out, token, sems = refs[n_marks:]
    copies = [
        pltpu.make_async_copy(base_ref, base_out, sems.at[0]),
        pltpu.make_async_copy(dual_ref, dual_out, sems.at[1]),
    ]
    for copy in copies:
        copy.start()
    token[...] = jnp.ones_like(token)
    for copy in copies:
        copy.wait()


def load(marks, base_weight, dual_start):
    anywhere = pl.BlockSpec(memory_space=pl.ANY)
    return pl.pallas_call(
        functools.partial(load_kernel, len(marks)),
        in_specs=[anywhere] * (len(marks) + 2),
        out_specs=[anywhere, anywhere, pl.BlockSpec(memory_space=pltpu.VMEM)],
        out_shape=[pltpu.VMEM(x.shape, x.dtype) for x in (base_weight, dual_start)]
        + [jax.ShapeDtypeStruct(marks[0].shape, BF16)],
        scratch_shapes=[pltpu.SemaphoreType.DMA((2,))],
        compiler_params=pltpu.CompilerParams(vmem_limit_bytes=16 * MIB),
        cost_estimate=pl.CostEstimate(flops=0, bytes_accessed=6 * base_weight.size, transcendentals=0),
    )(*marks, base_weight, dual_start)


def fused_kernel(chunk, topk, halves, *refs):
    gathered = refs[:halves]
    base_ref, _, keep_ref, weight_hbm, dual_hbm, dual, *refs = refs[halves:]
    rows, held, rank, hits, mask, weight_sems, dual_sems = refs
    expert = pl.program_id(0)
    tokens = gathered[0].shape[0]
    slots, width = rows.shape
    part_width = width // halves
    local, tall, _ = base_ref.shape
    cuts = cuts_of(width, chunk)
    parts = [slice(start, start + BLOCK) for start in range(0, tall, BLOCK)]

    def weight_copy(at, i):
        return pltpu.make_async_copy(held.at[:, cuts[i]], weight_hbm.at[at, :, cuts[i]], weight_sems.at[i])

    def dual_copy(at, i):
        return pltpu.make_async_copy(dual.at[at, :, cuts[i]], dual_hbm.at[at, :, cuts[i]], dual_sems.at[at, i])

    @pl.when(expert == 0)
    def _():
        named = gathered[0][:, pl.ds(part_width, LANES)].astype(F32).T[:topk, :]
        for own in range(local):
            label = (lax.axis_index("exp") * local + own).astype(F32)
            hits[own : own + 1, :] = jnp.max(jnp.where(named == label, 1.0, 0.0), axis=0, keepdims=True)
        earlier = lax.broadcasted_iota(jnp.int32, (tokens, tokens), 0)
        later = lax.broadcasted_iota(jnp.int32, (tokens, tokens), 1)
        ahead = jnp.where(earlier < later, 1.0, 0.0).astype(BF16)
        rank[...] = dot_nn(hits[...].astype(BF16), ahead)
        count = keep_ref.shape[2]
        at = lax.broadcasted_iota(jnp.int32, (count, width), 0) * BLOCK
        column = lax.broadcasted_iota(jnp.int32, (count, width), 1)
        wide = jnp.where((column >= at) & (column < at + BLOCK), 1.0, 0.0).astype(BF16)
        for own in range(local):
            mask[own] = dot_nn(keep_ref[own].astype(F32).astype(BF16), wide)

    hit = hits[pl.ds(expert, 1), :]
    place = rank[pl.ds(expert, 1), :]
    slot = lax.broadcasted_iota(jnp.int32, (slots, tokens), 0).astype(F32)
    taken = jnp.where((slot == place) & (hit > 0.5), 1.0, 0.0).astype(BF16)
    rate = step_rate / jnp.sum(hit, axis=1, keepdims=True)
    resid = jnp.zeros((tall, slots), F32)
    for cut in cuts:
        half, start = divmod(cut.start, part_width)
        rows[:, cut] = dot_nn(taken, gathered[half][:, pl.ds(start, chunk)]).astype(BF16)
        deltas = [
            base_ref[expert, part, cut] * (mask[expert, i : i + 1, cut] - 1.0).astype(BF16) for i, part in enumerate(parts)
        ]
        resid = resid + dot_nt(jnp.concatenate(deltas, axis=0), rows[:, cut])
    resid = resid.astype(BF16)

    @pl.when(expert > 0)
    def _():
        for i in range(len(cuts)):
            weight_copy(expert - 1, i).wait()

    after = jnp.zeros((tall, slots), F32)
    for cut in cuts:
        grad = dot_nn(resid, rows[:, cut])
        deltas = []
        for i, part in enumerate(parts):
            base = base_ref[expert, part, cut].astype(F32)
            weight = mask[expert, i : i + 1, cut] * base - step_rate * dual[expert, part, cut] - rate * grad[part, :]
            held[part, cut] = weight
            deltas.append((weight - base).astype(BF16))
        after = after + dot_nt(jnp.concatenate(deltas, axis=0), rows[:, cut])
    resid = after.astype(BF16)

    for n, cut in enumerate(cuts):
        grad = dot_nn(resid, rows[:, cut])
        for i, part in enumerate(parts):
            keep = mask[expert, i : i + 1, cut]
            weight = held[part, cut]
            both = weight + dual[expert, part, cut]
            weight = (1.0 - step_rate) * weight - (step_rate - 2.0 * step_rate * keep) * both - rate * grad[part, :]
            held[part, cut] = weight
            dual[expert, part, cut] = (1.0 - keep) * (both + weight)
        weight_copy(expert, n).start()
        dual_copy(expert, n).start()

    @pl.when(expert == local - 1)
    def _():
        for i in range(len(cuts)):
            weight_copy(expert, i).wait()
        for at in range(local):
            for i in range(len(cuts)):
                dual_copy(at, i).wait()


def fused(gathered, base_weight, keep_mask, dual_start, topk):
    local, tall, width = base_weight.shape
    chunk = 512
    tokens = gathered[0].shape[0]
    slots = min(-(-tokens // ROWS_BLOCK) * MOST, tokens)
    slots = -(-slots // LANES) * LANES
    whole = pl.BlockSpec(memory_space=pltpu.VMEM)
    anywhere = pl.BlockSpec(memory_space=pl.ANY)
    out = jax.ShapeDtypeStruct(dual_start.shape, F32)
    macs = local * slots * width * (4 * tall + tokens)
    scoped = 4 * tall * width + 2 * slots * (width + 2 * tokens) + SPARE * MIB
    held = [pltpu.with_memory_space_constraint(x, pltpu.VMEM) for x in (*gathered, base_weight, dual_start)]
    outs = pl.pallas_call(
        functools.partial(fused_kernel, chunk, topk, len(gathered)),
        grid=(local,),
        in_specs=[whole] * (len(held) + 1),
        out_specs=[anywhere, anywhere, whole],
        out_shape=[out, out, pltpu.VMEM(dual_start.shape, F32)],
        input_output_aliases={len(held) - 1: 2},
        scratch_shapes=[
            pltpu.VMEM((slots, width), BF16),
            pltpu.VMEM((tall, width), F32),
            pltpu.VMEM((local, tokens), F32),
            pltpu.VMEM((local, tokens), F32),
            pltpu.VMEM((local, keep_mask.shape[1], width), F32),
            pltpu.SemaphoreType.DMA((width // chunk,)),
            pltpu.SemaphoreType.DMA((local, width // chunk)),
        ],
        compiler_params=pltpu.CompilerParams(vmem_limit_bytes=scoped, dimension_semantics=("arbitrary",)),
        cost_estimate=pl.CostEstimate(flops=2 * macs, bytes_accessed=8 * base_weight.size, transcendentals=0),
    )(*held, keep_mask)
    return outs[0], outs[1]


def plain(gathered, base_weight, keep_mask, dual, topk):
    local, _, width = base_weight.shape
    part = width // len(gathered)
    routes = gathered[0][:, part : part + topk].astype(jnp.int32)
    rows = jnp.concatenate([piece[:, :part] for piece in gathered], axis=1)
    tokens = rows.shape[0]
    slots = min(-(-tokens // ROWS_BLOCK) * MOST, tokens)
    labels = lax.axis_index("exp") * local + jnp.arange(local, dtype=jnp.int32)
    hits = jnp.any(routes[:, :, None] == labels, axis=1)
    rank = jnp.cumsum(hits.astype(jnp.int32), axis=0) - 1
    taken = hits[:, :, None] & (rank[:, :, None] == jnp.arange(slots, dtype=jnp.int32))
    picked = jnp.einsum("rls,rd->lsd", taken.astype(BF16), rows, preferred_element_type=F32).astype(BF16)
    rate = (step_rate / jnp.sum(hits.astype(F32), axis=0))[:, None, None]
    mask = jnp.repeat(jnp.repeat(keep_mask.astype(F32), BLOCK, 1), BLOCK, 2)
    base = base_weight.astype(F32)
    weight = zed = mask * base
    for _ in range(ITERS):
        delta = (weight - base).astype(BF16)
        resid = jnp.einsum("lnd,lcd->lcn", picked, delta, preferred_element_type=F32).astype(BF16)
        grad = jnp.einsum("lcn,lnd->lcd", resid, picked, preferred_element_type=F32)
        weight = weight - rate * grad - step_rate * (weight - zed + dual)
        zed = mask * (weight + dual)
        dual = dual + weight - zed
    return weight, dual


def after(ones, array):
    return array * ones[: array.shape[0], : array.shape[1]]


def swap(piece, bit):
    n = lax.axis_size("exp")
    return lax.ppermute(piece, "exp", [(i, i ^ (1 << bit)) for i in range(n)])


def column_rows(own):
    n = lax.axis_size("tok")
    column = [own]
    for shift in range(1, n):
        column.append(lax.ppermute(own, "tok", [(i, (i + shift) % n) for i in range(n)]))
    return jnp.concatenate(column, axis=0)


def on_device(x_rows, routes, base_weight, keep_mask, dual_start):
    local, hidden, width = base_weight.shape
    topk = routes.shape[1]
    n_exp = lax.axis_size("exp")
    top = n_exp.bit_length() - 1
    assert 1 << top == n_exp
    halves = 2
    part = width // halves
    named = jnp.pad(routes.astype(BF16), ((0, 0), (0, LANES - topk)))
    sent = [x_rows[:, h * part : (h + 1) * part] for h in range(halves)]
    sent[0] = jnp.concatenate([sent[0], named], axis=1)
    with jax.named_scope("exchange_rows"):
        mine = [column_rows(own) for own in sent]
    if top != 3 or 2 * n_exp * mine[0].shape[0] * width > 16 * MIB:
        gathered = []
        for own in mine:
            pieces = {0: own}
            for bit in [*range(1, top), 0]:
                pieces.update({at ^ (1 << bit): swap(piece, bit) for at, piece in pieces.items()})
            gathered.append(jnp.concatenate([pieces[i] for i in range(n_exp)], axis=0))
        return plain(gathered, base_weight, keep_mask, dual_start, topk)
    with jax.named_scope("load_weights"):
        base_weight, dual_start, token = load(mine, base_weight, dual_start)
    gathered = []
    with jax.named_scope("exchange_rows"):
        near = [[own, swap(own, 1), swap(own, 2)] for own in mine]
        far = [swap(after(token, near[0][1]), 2), swap(after(token, near[1][2]), 1)]
        for blocks, last in zip(near, far):
            pieces = [*blocks, last]
            others = [swap(piece, 0) for piece in (after(token, blocks[0]), *pieces[1:])]
            gathered.append(jnp.concatenate(pieces + others, axis=0))
    with jax.named_scope("fused_iterations"):
        return fused(gathered, base_weight, keep_mask, dual_start, topk)


def solution(mesh):
    return jax.shard_map(
        on_device,
        mesh=mesh,
        in_specs=(
            P(("tok", "exp"), None),
            P(("tok", "exp"), None),
            P("exp", "tok", None),
            P("exp", "tok", None),
            P("exp", "tok", None),
        ),
        out_specs=(P("exp", "tok", None), P("exp", "tok", None)),
        check_vma=False,
    )
```

```python
import functools

import jax
import jax.numpy as jnp
from jax import lax
from jax.experimental import pallas as pl
from jax.experimental.pallas import tpu as pltpu
from jax.sharding import PartitionSpec as P

EXPERTS = 32
BLOCK = 64
ROWS_BLOCK = 24
MOST = 7
ITERS = 2
LANES = 128
MIB = 1024 * 1024
SPARE = 6

step_rate = 0.2

F32 = jnp.float32
BF16 = jnp.bfloat16


def dot_nn(a, b):
    return jnp.dot(a, b, preferred_element_type=F32)


def dot_nt(a, b):
    return lax.dot_general(a, b, (((1,), (1,)), ((), ())), preferred_element_type=F32)


def cuts_of(width, chunk):
    return [pl.ds(start, chunk) for start in range(0, width, chunk)]


def load_kernel(n_marks, *refs):
    base_ref, dual_ref, base_out, dual_out, token, sems = refs[n_marks:]
    copies = [
        pltpu.make_async_copy(base_ref, base_out, sems.at[0]),
        pltpu.make_async_copy(dual_ref, dual_out, sems.at[1]),
    ]
    for copy in copies:
        copy.start()
    token[...] = jnp.ones_like(token)
    for copy in copies:
        copy.wait()


def load(marks, base_weight, dual_start):
    anywhere = pl.BlockSpec(memory_space=pl.ANY)
    return pl.pallas_call(
        functools.partial(load_kernel, len(marks)),
        in_specs=[anywhere] * (len(marks) + 2),
        out_specs=[anywhere, anywhere, pl.BlockSpec(memory_space=pltpu.VMEM)],
        out_shape=[pltpu.VMEM(x.shape, x.dtype) for x in (base_weight, dual_start)]
        + [jax.ShapeDtypeStruct(marks[0].shape, BF16)],
        scratch_shapes=[pltpu.SemaphoreType.DMA((2,))],
        compiler_params=pltpu.CompilerParams(vmem_limit_bytes=16 * MIB),
        cost_estimate=pl.CostEstimate(flops=0, bytes_accessed=6 * base_weight.size, transcendentals=0),
    )(*marks, base_weight, dual_start)


def fused_kernel(chunk, topk, halves, *refs):
    gathered = refs[:halves]
    base_ref, _, keep_ref, weight_hbm, dual_hbm, dual, *refs = refs[halves:]
    rows, held, rank, hits, mask, weight_sems, dual_sems = refs
    expert = pl.program_id(0)
    tokens = gathered[0].shape[0]
    slots, width = rows.shape
    part_width = width // halves
    local, tall, _ = base_ref.shape
    cuts = cuts_of(width, chunk)
    parts = [slice(start, start + BLOCK) for start in range(0, tall, BLOCK)]

    def weight_copy(at, i):
        return pltpu.make_async_copy(held.at[:, cuts[i]], weight_hbm.at[at, :, cuts[i]], weight_sems.at[i])

    def dual_copy(at, i):
        return pltpu.make_async_copy(dual.at[at, :, cuts[i]], dual_hbm.at[at, :, cuts[i]], dual_sems.at[at, i])

    @pl.when(expert == 0)
    def _():
        named = gathered[0][:, pl.ds(part_width, LANES)].astype(F32).T[:topk, :]
        for own in range(local):
            label = (lax.axis_index("exp") * local + own).astype(F32)
            hits[own : own + 1, :] = jnp.max(jnp.where(named == label, 1.0, 0.0), axis=0, keepdims=True)
        earlier = lax.broadcasted_iota(jnp.int32, (tokens, tokens), 0)
        later = lax.broadcasted_iota(jnp.int32, (tokens, tokens), 1)
        ahead = jnp.where(earlier < later, 1.0, 0.0).astype(BF16)
        rank[...] = dot_nn(hits[...].astype(BF16), ahead)
        count = keep_ref.shape[2]
        at = lax.broadcasted_iota(jnp.int32, (count, width), 0) * BLOCK
        column = lax.broadcasted_iota(jnp.int32, (count, width), 1)
        wide = jnp.where((column >= at) & (column < at + BLOCK), 1.0, 0.0).astype(BF16)
        for own in range(local):
            mask[own] = dot_nn(keep_ref[own].astype(F32).astype(BF16), wide)

    hit = hits[pl.ds(expert, 1), :]
    place = rank[pl.ds(expert, 1), :]
    slot = lax.broadcasted_iota(jnp.int32, (slots, tokens), 0).astype(F32)
    taken = jnp.where((slot == place) & (hit > 0.5), 1.0, 0.0).astype(BF16)
    rate = step_rate / jnp.sum(hit, axis=1, keepdims=True)
    resid = jnp.zeros((tall, slots), F32)
    for cut in cuts:
        half, start = divmod(cut.start, part_width)
        rows[:, cut] = dot_nn(taken, gathered[half][:, pl.ds(start, chunk)]).astype(BF16)
        deltas = [
            base_ref[expert, part, cut] * (mask[expert, i : i + 1, cut] - 1.0).astype(BF16) for i, part in enumerate(parts)
        ]
        resid = resid + dot_nt(jnp.concatenate(deltas, axis=0), rows[:, cut])
    resid = resid.astype(BF16)

    @pl.when(expert > 0)
    def _():
        for i in range(len(cuts)):
            weight_copy(expert - 1, i).wait()

    after = jnp.zeros((tall, slots), F32)
    for cut in cuts:
        grad = dot_nn(resid, rows[:, cut])
        deltas = []
        for i, part in enumerate(parts):
            base = base_ref[expert, part, cut].astype(F32)
            weight = mask[expert, i : i + 1, cut] * base - step_rate * dual[expert, part, cut] - rate * grad[part, :]
            held[part, cut] = weight
            deltas.append((weight - base).astype(BF16))
        after = after + dot_nt(jnp.concatenate(deltas, axis=0), rows[:, cut])
    resid = after.astype(BF16)

    for n, cut in enumerate(cuts):
        grad = dot_nn(resid, rows[:, cut])
        for i, part in enumerate(parts):
            keep = mask[expert, i : i + 1, cut]
            weight = held[part, cut]
            both = weight + dual[expert, part, cut]
            weight = (1.0 - step_rate) * weight - (step_rate - 2.0 * step_rate * keep) * both - rate * grad[part, :]
            held[part, cut] = weight
            dual[expert, part, cut] = (1.0 - keep) * (both + weight)
        weight_copy(expert, n).start()
        dual_copy(expert, n).start()

    @pl.when(expert == local - 1)
    def _():
        for i in range(len(cuts)):
            weight_copy(expert, i).wait()
        for at in range(local):
            for i in range(len(cuts)):
                dual_copy(at, i).wait()


def fused(gathered, base_weight, keep_mask, dual_start, topk):
    local, tall, width = base_weight.shape
    chunk = 512
    tokens = gathered[0].shape[0]
    slots = min(-(-tokens // ROWS_BLOCK) * MOST, tokens)
    slots = -(-slots // LANES) * LANES
    whole = pl.BlockSpec(memory_space=pltpu.VMEM)
    anywhere = pl.BlockSpec(memory_space=pl.ANY)
    out = jax.ShapeDtypeStruct(dual_start.shape, F32)
    macs = local * slots * width * (4 * tall + tokens)
    scoped = 4 * tall * width + 2 * slots * (width + 2 * tokens) + SPARE * MIB
    held = [pltpu.with_memory_space_constraint(x, pltpu.VMEM) for x in (*gathered, base_weight, dual_start)]
    outs = pl.pallas_call(
        functools.partial(fused_kernel, chunk, topk, len(gathered)),
        grid=(local,),
        in_specs=[whole] * (len(held) + 1),
        out_specs=[anywhere, anywhere, whole],
        out_shape=[out, out, pltpu.VMEM(dual_start.shape, F32)],
        input_output_aliases={len(held) - 1: 2},
        scratch_shapes=[
            pltpu.VMEM((slots, width), BF16),
            pltpu.VMEM((tall, width), F32),
            pltpu.VMEM((local, tokens), F32),
            pltpu.VMEM((local, tokens), F32),
            pltpu.VMEM((local, keep_mask.shape[1], width), F32),
            pltpu.SemaphoreType.DMA((width // chunk,)),
            pltpu.SemaphoreType.DMA((local, width // chunk)),
        ],
        compiler_params=pltpu.CompilerParams(vmem_limit_bytes=scoped, dimension_semantics=("arbitrary",)),
        cost_estimate=pl.CostEstimate(flops=2 * macs, bytes_accessed=8 * base_weight.size, transcendentals=0),
    )(*held, keep_mask)
    return outs[0], outs[1]


def plain(gathered, base_weight, keep_mask, dual, topk):
    local, _, width = base_weight.shape
    part = width // len(gathered)
    routes = gathered[0][:, part : part + topk].astype(jnp.int32)
    rows = jnp.concatenate([piece[:, :part] for piece in gathered], axis=1)
    tokens = rows.shape[0]
    slots = min(-(-tokens // ROWS_BLOCK) * MOST, tokens)
    labels = lax.axis_index("exp") * local + jnp.arange(local, dtype=jnp.int32)
    hits = jnp.any(routes[:, :, None] == labels, axis=1)
    rank = jnp.cumsum(hits.astype(jnp.int32), axis=0) - 1
    taken = hits[:, :, None] & (rank[:, :, None] == jnp.arange(slots, dtype=jnp.int32))
    picked = jnp.einsum("rls,rd->lsd", taken.astype(BF16), rows, preferred_element_type=F32).astype(BF16)
    rate = (step_rate / jnp.sum(hits.astype(F32), axis=0))[:, None, None]
    mask = jnp.repeat(jnp.repeat(keep_mask.astype(F32), BLOCK, 1), BLOCK, 2)
    base = base_weight.astype(F32)
    weight = zed = mask * base
    for _ in range(ITERS):
        delta = (weight - base).astype(BF16)
        resid = jnp.einsum("lnd,lcd->lcn", picked, delta, preferred_element_type=F32).astype(BF16)
        grad = jnp.einsum("lcn,lnd->lcd", resid, picked, preferred_element_type=F32)
        weight = weight - rate * grad - step_rate * (weight - zed + dual)
        zed = mask * (weight + dual)
        dual = dual + weight - zed
    return weight, dual


def after(ones, array):
    return array * ones[: array.shape[0], : array.shape[1]]


def swap(piece, bit):
    n = lax.axis_size("exp")
    return lax.ppermute(piece, "exp", [(i, i ^ (1 << bit)) for i in range(n)])


def column_rows(own):
    n = lax.axis_size("tok")
    column = [own]
    for shift in range(1, n):
        column.append(lax.ppermute(own, "tok", [(i, (i + shift) % n) for i in range(n)]))
    return jnp.concatenate(column, axis=0)


def on_device(x_rows, routes, base_weight, keep_mask, dual_start):
    local, hidden, width = base_weight.shape
    topk = routes.shape[1]
    n_exp = lax.axis_size("exp")
    top = n_exp.bit_length() - 1
    assert 1 << top == n_exp
    halves = 2
    part = width // halves
    named = jnp.pad(routes.astype(BF16), ((0, 0), (0, LANES - topk)))
    sent = [x_rows[:, h * part : (h + 1) * part] for h in range(halves)]
    sent[0] = jnp.concatenate([sent[0], named], axis=1)
    with jax.named_scope("exchange_rows"):
        mine = [column_rows(own) for own in sent]
    if top != 3 or 2 * n_exp * mine[0].shape[0] * width > 16 * MIB:
        gathered = []
        for own in mine:
            pieces = {0: own}
            for bit in [*range(1, top), 0]:
                pieces.update({at ^ (1 << bit): swap(piece, bit) for at, piece in pieces.items()})
            gathered.append(jnp.concatenate([pieces[i] for i in range(n_exp)], axis=0))
        return plain(gathered, base_weight, keep_mask, dual_start, topk)
    with jax.named_scope("load_weights"):
        base_weight, dual_start, token = load(mine, base_weight, dual_start)
    gathered = []
    with jax.named_scope("exchange_rows"):
        near = [[own, swap(own, 1), swap(own, 2)] for own in mine]
        far = [swap(after(token, near[0][1]), 2), swap(after(token, near[1][2]), 1)]
        for h, ((own, *others), last) in enumerate(zip(near, far)):
            pair = swap(jnp.concatenate([after(token, others[0]), others[1]], axis=0), 0)
            theirs = [swap(own if h else after(token, own), 0), pair, swap(last, 0)]
            gathered.append(jnp.concatenate([own, *others, last, *theirs], axis=0))
    with jax.named_scope("fused_iterations"):
        return fused(gathered, base_weight, keep_mask, dual_start, topk)


def solution(mesh):
    return jax.shard_map(
        on_device,
        mesh=mesh,
        in_specs=(
            P(("tok", "exp"), None),
            P(("tok", "exp"), None),
            P("exp", "tok", None),
            P("exp", "tok", None),
            P("exp", "tok", None),
        ),
        out_specs=(P("exp", "tok", None), P("exp", "tok", None)),
        check_vma=False,
    )
```

```python
import functools

import jax
import jax.numpy as jnp
from jax import lax
from jax.experimental import pallas as pl
from jax.experimental.pallas import tpu as pltpu
from jax.sharding import PartitionSpec as P

EXPERTS = 32
BLOCK = 64
ROWS_BLOCK = 24
MOST = 7
ITERS = 2
LANES = 128
MIB = 1024 * 1024
SPARE = 6

step_rate = 0.2

F32 = jnp.float32
BF16 = jnp.bfloat16


def dot_nn(a, b):
    return jnp.dot(a, b, preferred_element_type=F32)


def dot_nt(a, b):
    return lax.dot_general(a, b, (((1,), (1,)), ((), ())), preferred_element_type=F32)


def cuts_of(width, chunk):
    return [pl.ds(start, chunk) for start in range(0, width, chunk)]


def load_kernel(n_marks, *refs):
    base_ref, dual_ref, base_out, dual_out, token, sems = refs[n_marks:]
    copies = [
        pltpu.make_async_copy(base_ref, base_out, sems.at[0]),
        pltpu.make_async_copy(dual_ref, dual_out, sems.at[1]),
    ]
    for copy in copies:
        copy.start()
    token[...] = jnp.ones_like(token)
    for copy in copies:
        copy.wait()


def load(marks, base_weight, dual_start):
    anywhere = pl.BlockSpec(memory_space=pl.ANY)
    return pl.pallas_call(
        functools.partial(load_kernel, len(marks)),
        in_specs=[anywhere] * (len(marks) + 2),
        out_specs=[anywhere, anywhere, pl.BlockSpec(memory_space=pltpu.VMEM)],
        out_shape=[pltpu.VMEM(x.shape, x.dtype) for x in (base_weight, dual_start)]
        + [jax.ShapeDtypeStruct(marks[0].shape, BF16)],
        scratch_shapes=[pltpu.SemaphoreType.DMA((2,))],
        compiler_params=pltpu.CompilerParams(vmem_limit_bytes=16 * MIB),
        cost_estimate=pl.CostEstimate(flops=0, bytes_accessed=6 * base_weight.size, transcendentals=0),
    )(*marks, base_weight, dual_start)


def fused_kernel(chunk, topk, halves, *refs):
    gathered = refs[:halves]
    base_ref, _, keep_ref, weight_hbm, dual_hbm, dual, *refs = refs[halves:]
    rows, held, rank, hits, mask, weight_sems, dual_sems = refs
    expert = pl.program_id(0)
    tokens = gathered[0].shape[0]
    slots, width = rows.shape
    part_width = width // halves
    local, tall, _ = base_ref.shape
    cuts = cuts_of(width, chunk)
    parts = [slice(start, start + BLOCK) for start in range(0, tall, BLOCK)]

    def weight_copy(at, i):
        return pltpu.make_async_copy(held.at[:, cuts[i]], weight_hbm.at[at, :, cuts[i]], weight_sems.at[i])

    def dual_copy(at, i):
        return pltpu.make_async_copy(dual.at[at, :, cuts[i]], dual_hbm.at[at, :, cuts[i]], dual_sems.at[at, i])

    @pl.when(expert == 0)
    def _():
        named = gathered[0][:, pl.ds(part_width, LANES)].astype(F32).T[:topk, :]
        for own in range(local):
            label = (lax.axis_index("exp") * local + own).astype(F32)
            hits[own : own + 1, :] = jnp.max(jnp.where(named == label, 1.0, 0.0), axis=0, keepdims=True)
        earlier = lax.broadcasted_iota(jnp.int32, (tokens, tokens), 0)
        later = lax.broadcasted_iota(jnp.int32, (tokens, tokens), 1)
        ahead = jnp.where(earlier < later, 1.0, 0.0).astype(BF16)
        rank[...] = dot_nn(hits[...].astype(BF16), ahead)
        count = keep_ref.shape[2]
        at = lax.broadcasted_iota(jnp.int32, (count, width), 0) * BLOCK
        column = lax.broadcasted_iota(jnp.int32, (count, width), 1)
        wide = jnp.where((column >= at) & (column < at + BLOCK), 1.0, 0.0).astype(BF16)
        for own in range(local):
            mask[own] = dot_nn(keep_ref[own].astype(F32).astype(BF16), wide)

    hit = hits[pl.ds(expert, 1), :]
    place = rank[pl.ds(expert, 1), :]
    slot = lax.broadcasted_iota(jnp.int32, (slots, tokens), 0).astype(F32)
    taken = jnp.where((slot == place) & (hit > 0.5), 1.0, 0.0).astype(BF16)
    rate = step_rate / jnp.sum(hit, axis=1, keepdims=True)
    resid = jnp.zeros((tall, slots), F32)
    for cut in cuts:
        half, start = divmod(cut.start, part_width)
        rows[:, cut] = dot_nn(taken, gathered[half][:, pl.ds(start, chunk)]).astype(BF16)
        deltas = [
            base_ref[expert, part, cut] * (mask[expert, i : i + 1, cut] - 1.0).astype(BF16) for i, part in enumerate(parts)
        ]
        resid = resid + dot_nt(jnp.concatenate(deltas, axis=0), rows[:, cut])
    resid = resid.astype(BF16)

    @pl.when(expert > 0)
    def _():
        for i in range(len(cuts)):
            weight_copy(expert - 1, i).wait()

    after = jnp.zeros((tall, slots), F32)
    for cut in cuts:
        grad = dot_nn(resid, rows[:, cut])
        deltas = []
        for i, part in enumerate(parts):
            base = base_ref[expert, part, cut].astype(F32)
            weight = mask[expert, i : i + 1, cut] * base - step_rate * dual[expert, part, cut] - rate * grad[part, :]
            held[part, cut] = weight
            deltas.append((weight - base).astype(BF16))
        after = after + dot_nt(jnp.concatenate(deltas, axis=0), rows[:, cut])
    resid = after.astype(BF16)

    for n, cut in enumerate(cuts):
        grad = dot_nn(resid, rows[:, cut])
        for i, part in enumerate(parts):
            keep = mask[expert, i : i + 1, cut]
            weight = held[part, cut]
            both = weight + dual[expert, part, cut]
            weight = (1.0 - step_rate) * weight - (step_rate - 2.0 * step_rate * keep) * both - rate * grad[part, :]
            held[part, cut] = weight
            dual[expert, part, cut] = (1.0 - keep) * (both + weight)
        weight_copy(expert, n).start()
        dual_copy(expert, n).start()

    @pl.when(expert == local - 1)
    def _():
        for i in range(len(cuts)):
            weight_copy(expert, i).wait()
        for at in range(local):
            for i in range(len(cuts)):
                dual_copy(at, i).wait()


def fused(gathered, base_weight, keep_mask, dual_start, topk):
    local, tall, width = base_weight.shape
    chunk = 256
    tokens = gathered[0].shape[0]
    slots = min(-(-tokens // ROWS_BLOCK) * MOST, tokens)
    slots = -(-slots // LANES) * LANES
    whole = pl.BlockSpec(memory_space=pltpu.VMEM)
    anywhere = pl.BlockSpec(memory_space=pl.ANY)
    out = jax.ShapeDtypeStruct(dual_start.shape, F32)
    macs = local * slots * width * (4 * tall + tokens)
    scoped = 4 * tall * width + 2 * slots * (width + 2 * tokens) + SPARE * MIB
    held = [pltpu.with_memory_space_constraint(x, pltpu.VMEM) for x in (*gathered, base_weight, dual_start)]
    outs = pl.pallas_call(
        functools.partial(fused_kernel, chunk, topk, len(gathered)),
        grid=(local,),
        in_specs=[whole] * (len(held) + 1),
        out_specs=[anywhere, anywhere, whole],
        out_shape=[out, out, pltpu.VMEM(dual_start.shape, F32)],
        input_output_aliases={len(held) - 1: 2},
        scratch_shapes=[
            pltpu.VMEM((slots, width), BF16),
            pltpu.VMEM((tall, width), F32),
            pltpu.VMEM((local, tokens), F32),
            pltpu.VMEM((local, tokens), F32),
            pltpu.VMEM((local, keep_mask.shape[1], width), F32),
            pltpu.SemaphoreType.DMA((width // chunk,)),
            pltpu.SemaphoreType.DMA((local, width // chunk)),
        ],
        compiler_params=pltpu.CompilerParams(vmem_limit_bytes=scoped, dimension_semantics=("arbitrary",)),
        cost_estimate=pl.CostEstimate(flops=2 * macs, bytes_accessed=8 * base_weight.size, transcendentals=0),
    )(*held, keep_mask)
    return outs[0], outs[1]


def plain(gathered, base_weight, keep_mask, dual, topk):
    local, _, width = base_weight.shape
    part = width // len(gathered)
    routes = gathered[0][:, part : part + topk].astype(jnp.int32)
    rows = jnp.concatenate([piece[:, :part] for piece in gathered], axis=1)
    tokens = rows.shape[0]
    slots = min(-(-tokens // ROWS_BLOCK) * MOST, tokens)
    labels = lax.axis_index("exp") * local + jnp.arange(local, dtype=jnp.int32)
    hits = jnp.any(routes[:, :, None] == labels, axis=1)
    rank = jnp.cumsum(hits.astype(jnp.int32), axis=0) - 1
    taken = hits[:, :, None] & (rank[:, :, None] == jnp.arange(slots, dtype=jnp.int32))
    picked = jnp.einsum("rls,rd->lsd", taken.astype(BF16), rows, preferred_element_type=F32).astype(BF16)
    rate = (step_rate / jnp.sum(hits.astype(F32), axis=0))[:, None, None]
    mask = jnp.repeat(jnp.repeat(keep_mask.astype(F32), BLOCK, 1), BLOCK, 2)
    base = base_weight.astype(F32)
    weight = zed = mask * base
    for _ in range(ITERS):
        delta = (weight - base).astype(BF16)
        resid = jnp.einsum("lnd,lcd->lcn", picked, delta, preferred_element_type=F32).astype(BF16)
        grad = jnp.einsum("lcn,lnd->lcd", resid, picked, preferred_element_type=F32)
        weight = weight - rate * grad - step_rate * (weight - zed + dual)
        zed = mask * (weight + dual)
        dual = dual + weight - zed
    return weight, dual


def after(ones, array):
    return array * ones[: array.shape[0], : array.shape[1]]


def swap(piece, bit):
    n = lax.axis_size("exp")
    return lax.ppermute(piece, "exp", [(i, i ^ (1 << bit)) for i in range(n)])


def column_rows(own):
    n = lax.axis_size("tok")
    column = [own]
    for shift in range(1, n):
        column.append(lax.ppermute(own, "tok", [(i, (i + shift) % n) for i in range(n)]))
    return jnp.concatenate(column, axis=0)


def on_device(x_rows, routes, base_weight, keep_mask, dual_start):
    local, hidden, width = base_weight.shape
    topk = routes.shape[1]
    n_exp = lax.axis_size("exp")
    top = n_exp.bit_length() - 1
    assert 1 << top == n_exp
    halves = 2
    part = width // halves
    named = jnp.pad(routes.astype(BF16), ((0, 0), (0, LANES - topk)))
    sent = [x_rows[:, h * part : (h + 1) * part] for h in range(halves)]
    sent[0] = jnp.concatenate([sent[0], named], axis=1)
    with jax.named_scope("exchange_rows"):
        mine = [column_rows(own) for own in sent]
    if top != 3 or 2 * n_exp * mine[0].shape[0] * width > 16 * MIB:
        gathered = []
        for own in mine:
            pieces = {0: own}
            for bit in [*range(1, top), 0]:
                pieces.update({at ^ (1 << bit): swap(piece, bit) for at, piece in pieces.items()})
            gathered.append(jnp.concatenate([pieces[i] for i in range(n_exp)], axis=0))
        return plain(gathered, base_weight, keep_mask, dual_start, topk)
    with jax.named_scope("load_weights"):
        base_weight, dual_start, token = load(mine, base_weight, dual_start)
    gathered = []
    with jax.named_scope("exchange_rows"):
        near = [[own, swap(own, 1), swap(own, 2)] for own in mine]
        far = [swap(after(token, near[0][1]), 2), swap(after(token, near[1][2]), 1)]
        for h, ((own, *others), last) in enumerate(zip(near, far)):
            pair = swap(jnp.concatenate([after(token, others[0]), others[1]], axis=0), 0)
            theirs = [swap(own if h else after(token, own), 0), pair, swap(last, 0)]
            gathered.append(jnp.concatenate([own, *others, last, *theirs], axis=0))
    with jax.named_scope("fused_iterations"):
        return fused(gathered, base_weight, keep_mask, dual_start, topk)


def solution(mesh):
    return jax.shard_map(
        on_device,
        mesh=mesh,
        in_specs=(
            P(("tok", "exp"), None),
            P(("tok", "exp"), None),
            P("exp", "tok", None),
            P("exp", "tok", None),
            P("exp", "tok", None),
        ),
        out_specs=(P("exp", "tok", None), P("exp", "tok", None)),
        check_vma=False,
    )
```
